256 devices in a mesh: bead: 8 (over z), space: 32 (over x, y, core).
Axes of the slice: x: 4, y: 4, z: 8, core: 2. Of those that a mesh axis runs over, the one named last changes fastest.
Arguments:
- positions: float32 [16, 3, 196608], P('bead', None, 'space'), may hold values from -0.6 to 8.6, as said below
- momenta: float32 [16, 3, 196608], P('bead', None, 'space'), may hold values from -6 to 6
- thermostat: float32 [16, 4, 3, 196608], P('bead', None, None, 'space'), may hold values from -3 to 3
- atom_types: int32 [196608], P('space'), may hold values from 0 to 127
- masses: float32 [128], replicated, may hold values from 1 to 16
- pair_table: bfloat16 [128, 128], replicated, may hold values from 0.5 to 2, as said below
- tile_pairs: int32 [32, 2, 672], P('space'), may hold values from 0 to 143, as said below
- tile_count: int32 [32], P('space'), may hold values from 336 to 672
- move_rows: int32 [32, 4, 96], P('space'), may hold values from 0 to 6143, as said below
- move_count: int32 [32, 4], P('space'), may hold values from 32 to 96, as said below
Outputs:
- positions_out: float32 [16, 3, 196608], P('bead', None, 'space')
- momenta_out: float32 [16, 3, 196608], P('bead', None, 'space')
- thermo_out: float32 [16, 4, 3, 196608], P('bead', None, None, 'space')
- forces: float32 [16, 3, 196608], P('bead', None, 'space')
- types_out: int32 [196608], P('space')
The draws below stay inside these ranges and needn't reach their ends.
Inputs may be any that keep to these rules, and one draw needn't show every extreme that they name: `positions`: slot s of a domain belongs to cell c = s // 128 at y index c // 6 and z index c % 6. `pair_table`: Symmetric. `tile_pairs`: row 0 holds a cell of the domain; row 1 a cell of its extended list: cells of the domain below (0 to 47), of the domain (48 to 95), of the domain above (96 to 143). Entries from tile_count on are padding with valid indices. `move_rows`: the rows listed by one domain are distinct over all four classes; entries from the class's count on are padding. `move_count`: column k counts the cycle polymers a domain sends (+1, -1, +2, -2)[k] domains away on the periodic axis. As many go from domain d to d + 1 as from d + 1 to d, and as many from d to d + 2 as from d + 2 to d.
All inputs are finite; a program needn't handle non-finite values.
Results may differ from the reference program's by a relative error of at most 0.0003.
Values sent between devices are 32-bit elements; how exact they have to be, the bound alone decides.
A program may use at most 128 MiB of HBM per device.

```python
import math
import jax
import jax.numpy as jnp
from jax import lax

NBEADS = 16
CAP = 128
CY = 8
CZ = 6
CELLS = 48
SLOTS = 6144
ATOMS = 196608
NTYPES = 128
CHAIN = 4
MCAP = 96
TILES = 672
N_SPACE = 32


def tile_layout(key):
    key = jax.random.fold_in(key, 31)
    count_key, order_key, full_key = jax.random.split(key, 3)
    domains = ATOMS // SLOTS
    cell_total = CY * CZ
    own_cell = jnp.arange(cell_total * 27, dtype=jnp.int32) // 27
    stencil = jnp.arange(cell_total * 27, dtype=jnp.int32) % 27
    shift_x = stencil // 9 - 1
    shift_y = stencil // 3 % 3 - 1
    shift_z = stencil % 3 - 1
    near_y = own_cell // CZ + shift_y
    near_z = own_cell % CZ + shift_z
    inside = (near_y >= 0) & (near_y < CY) & (near_z >= 0) & (near_z < CZ)
    target = (shift_x + 1) * cell_total + near_y * CZ + near_z

    def one_domain(domain_key):
        ranking = jax.random.permutation(domain_key, cell_total * 27).astype(jnp.int32)
        scores = jnp.where(inside, ranking, ranking + cell_total * 27)
        chosen = jnp.argsort(scores, stable=True)[:TILES]
        return jnp.stack([own_cell[chosen], target[chosen]])
    tile_ids = jax.vmap(one_domain)(jax.random.split(order_key, domains))
    live_counts = jax.random.randint(count_key, (domains,), TILES // 2, TILES + 1)
    fullest = jax.random.randint(full_key, (), 0, domains)
    live_counts = jnp.where(jnp.arange(domains) == fullest, TILES, live_counts)
    return (tile_ids.astype(jnp.int32), live_counts.astype(jnp.int32))


def migration_lists(key):
    key = jax.random.fold_in(key, 47)
    near_key, far_key, rows_key = jax.random.split(key, 3)
    domains = ATOMS // SLOTS

    def link_counts(link_key, lowest, highest_count):
        first_key, second_key = jax.random.split(link_key)
        drawn = jax.random.randint(first_key, (domains,), lowest, highest_count + 1)
        busiest = jax.random.randint(second_key, (), 0, domains)
        return jnp.where(jnp.arange(domains) == busiest, highest_count, drawn)
    near_flow = link_counts(near_key, MCAP // 3, MCAP)
    far_flow = link_counts(far_key, MCAP // 3, MCAP // 2)
    live_counts = jnp.stack([near_flow, jnp.roll(near_flow, 1), far_flow, jnp.roll(far_flow, 2)], axis=1)

    def domain_rows(row_key):
        return jax.random.permutation(row_key, SLOTS)[:4 * MCAP].reshape(4, MCAP)
    row_ids = jax.vmap(domain_rows)(jax.random.split(rows_key, domains))
    return (row_ids.astype(jnp.int32), live_counts.astype(jnp.int32))


def draw_positions(key, part):
    key = jax.random.fold_in(key, 1)
    centre_key, spread_key = jax.random.split(key)
    slot_index = jnp.arange(ATOMS, dtype=jnp.int32) % SLOTS
    cell_index = slot_index // CAP
    cell_y = (cell_index // CZ).astype(jnp.float32)
    cell_z = (cell_index % CZ).astype(jnp.float32)
    within = jax.random.uniform(centre_key, (3, ATOMS), jnp.float32)
    centre = within + jnp.stack([jnp.zeros_like(cell_y), cell_y, cell_z])
    spread = 0.15 * jnp.clip(jax.random.normal(spread_key, (NBEADS, 3, ATOMS), jnp.float32), -4.0, 4.0)
    return centre[None] + spread


def draw_pair_table(key, part):
    key = jax.random.fold_in(key, 2)
    raw_table = jax.random.uniform(key, (NTYPES, NTYPES), jnp.float32, 0.5, 2.0)
    return (0.5 * (raw_table + raw_table.T)).astype(jnp.bfloat16)


def draw_tile_pairs(key, part):
    shared = tile_layout(key)
    return shared[0]


def draw_tile_count(key, part):
    shared = tile_layout(key)
    return shared[1]


def draw_move_rows(key, part):
    shared = migration_lists(key)
    return shared[0]


def draw_move_count(key, part):
    shared = migration_lists(key)
    return shared[1]


def plant(values, rng, least, high):
    place = [jax.random.randint(jax.random.fold_in(rng, axis), (), 0, length) for axis, length in enumerate(values.shape)]
    widest = values.shape.index(max(values.shape))
    next_to = place[:widest] + [(place[widest] + 1) % values.shape[widest]] + place[widest + 1:]
    return values.at[tuple(place)].set(least).at[tuple(next_to)].set(high)


def block_scale(key, extent, shards, least, high):
    def one(dim, blocks):
        steps = jax.random.uniform(jax.random.fold_in(jax.random.fold_in(key, 6), dim), (blocks,), jnp.float32, least / len(shards), high / len(shards))
        return jnp.repeat(jnp.exp(steps), extent[dim] // blocks).reshape((-1,) + (1,) * (len(extent) - dim - 1))

    level = one(*shards[0])
    for cut in shards[1:]:
        level = level * one(*cut)
    return level


def noise(stream_key, shape, deviation, most, pieces=(), kind=jnp.bfloat16):
    values = jax.random.normal(stream_key, shape, jnp.float32) * deviation
    if len(pieces) > 0:
        values = block_scale(stream_key, shape, pieces, -0.22, 0.18) * values
    return jnp.clip(values, min=-most, max=most).astype(kind)


def setup_inputs(seed: int = 0) -> dict:
    streams_of = jax.random.split(jax.random.key(seed), 11)
    return {
        "positions": draw_positions(jax.random.fold_in(streams_of[10], 71), 0),
        "momenta": noise(streams_of[1], (NBEADS, 3, ATOMS), 1.0, 6.0, ((0, 8), (2, 32)), jnp.float32),
        "thermostat": noise(streams_of[2], (NBEADS, CHAIN, 3, ATOMS), 0.5, 3.0, ((0, 8), (3, 32)), jnp.float32),
        "atom_types": plant(jax.random.randint(streams_of[3], (ATOMS,), 0, NTYPES), jax.random.fold_in(streams_of[3], 1), 0, NTYPES - 1).astype(jnp.int32),
        "masses": jnp.clip(jnp.exp(jax.random.uniform(streams_of[4], (NTYPES,), jnp.float32, math.log(1.0), math.log(16.0))), 1.0, 16.0),
        "pair_table": draw_pair_table(jax.random.fold_in(streams_of[10], 71), 0),
        "tile_pairs": draw_tile_pairs(jax.random.fold_in(streams_of[10], 71), 0),
        "tile_count": draw_tile_count(jax.random.fold_in(streams_of[10], 71), 0),
        "move_rows": draw_move_rows(jax.random.fold_in(streams_of[10], 71), 0),
        "move_count": draw_move_count(jax.random.fold_in(streams_of[10], 71), 0),
    }


outer_step = 0.2
inner_step = 0.05
thermal = 1.0
chain_mass = 2.0
cycle_freq = 2.0
pair_reach = 0.4
slab_width = 1.0
offsets = (1, -1, 2, -2)
opposite = (1, 0, 3, 2)
tile_block = 56
highest = lax.Precision.HIGHEST


def chain_half(momenta, thermostat, atom_mass):
    half_step = 0.5 * outer_step
    levels = [thermostat[:, rung_index] for rung_index in range(thermostat.shape[1])]
    deepest = len(levels) - 1
    levels[deepest] = levels[deepest] + half_step * (chain_mass * levels[deepest - 1] * levels[deepest - 1] - thermal) / chain_mass
    for rung_index in range(deepest - 1, -1, -1):
        if rung_index == 0:
            driving = (momenta * momenta / atom_mass - thermal) / chain_mass
        else:
            driving = (chain_mass * levels[rung_index - 1] * levels[rung_index - 1] - thermal) / chain_mass
        levels[rung_index] = levels[rung_index] * jnp.exp(-levels[rung_index + 1] * half_step) + half_step * driving
    return momenta * jnp.exp(-levels[0] * half_step), jnp.stack(levels, axis=1)


def cycle_matrices(bead_total):
    mode_ids = jnp.arange(bead_total, dtype=jnp.int32)
    frequency = 2.0 * cycle_freq * jnp.sin(math.pi * mode_ids.astype(jnp.float32) / bead_total)
    rotation = frequency * outer_step
    moving = mode_ids > 0
    safe_freq = jnp.where(moving, frequency, 1.0)
    forward_map = jnp.where(moving, jnp.sin(rotation) / safe_freq, outer_step)
    backward = -frequency * jnp.sin(rotation)
    cosine = jnp.cos(rotation)
    bead_lag = (mode_ids[:, None] - mode_ids[None, :]) % bead_total
    phases = jnp.cos((2.0 * math.pi / bead_total) * ((bead_lag[:, :, None] * mode_ids[None, None, :]) % bead_total).astype(jnp.float32))

    def circulant(values):
        return jnp.sum(phases * values, axis=2) / bead_total

    return jnp.stack([jnp.stack([circulant(cosine), circulant(forward_map)]), jnp.stack([circulant(backward), circulant(cosine)])])


def reference(positions, momenta, thermostat, atom_types, masses, pair_table, tile_pairs, tile_count, move_rows, move_count):
    domains = N_SPACE
    atom_mass = masses[atom_types]
    momenta_half, thermo_half = chain_half(momenta, thermostat, atom_mass)
    velocity = momenta_half / atom_mass
    matrix = cycle_matrices(NBEADS)
    stacked = jnp.stack([positions, velocity], axis=1)
    moved_pair = jnp.einsum("xyjn,nyca->jxca", matrix, stacked, precision=highest)
    drifted = moved_pair[:, 0]
    momenta_drift = moved_pair[:, 1] * atom_mass

    channels = 6 + 3 * CHAIN
    payload = jnp.concatenate([drifted, momenta_drift, thermo_half.reshape(NBEADS, 3 * CHAIN, ATOMS)], axis=1)
    payload = payload.reshape(NBEADS, channels, domains, SLOTS)
    kind_grid = atom_types.reshape(domains, SLOTS)
    result = payload
    kinds_out = kind_grid
    domain_ids = jnp.arange(domains, dtype=jnp.int32)
    slot_order = jnp.arange(MCAP, dtype=jnp.int32)
    for class_index in range(4):
        source = (domain_ids - offsets[class_index]) % domains
        from_rows = move_rows[source, class_index]
        live_mask = slot_order[None, :] < move_count[:, opposite[class_index]][:, None]
        into_rows = jnp.where(live_mask, move_rows[:, opposite[class_index]], SLOTS)
        leaving = payload[:, :, source[:, None], from_rows]
        leaving = leaving.at[:, 0].add(-offsets[class_index] * slab_width)
        result = result.at[:, :, domain_ids[:, None], into_rows].set(leaving, mode="drop")
        kinds_out = kinds_out.at[domain_ids[:, None], into_rows].set(kind_grid[source[:, None], from_rows], mode="drop")
    flat_state = result.reshape(NBEADS, channels, ATOMS)
    positions_out = flat_state[:, :3]
    momenta_moved = flat_state[:, 3:6]
    thermo_out = flat_state[:, 6:].reshape(NBEADS, CHAIN, 3, ATOMS)
    types_out = kinds_out.reshape(ATOMS)

    cell_grid = positions_out.reshape(NBEADS, 3, domains, CELLS, CAP)
    type_grid = types_out.reshape(domains, CELLS, CAP)
    frame_shift = jnp.repeat(jnp.array([-slab_width, 0.0, slab_width], dtype=jnp.float32), CELLS)
    inverse_width = 0.5 / (pair_reach * pair_reach)
    pair_scale = 1.0 / (pair_reach * pair_reach * NBEADS)

    def domain_forces(domain):
        lower_side = (domain - 1) % domains
        upper_side = (domain + 1) % domains
        own_cells = cell_grid[:, :, domain]
        extended = jnp.concatenate([cell_grid[:, :, lower_side], own_cells, cell_grid[:, :, upper_side]], axis=2)
        extended = extended.at[:, 0].add(frame_shift[:, None])
        own_types = type_grid[domain]
        wide_types = jnp.concatenate([type_grid[lower_side], own_types, type_grid[upper_side]], axis=0)
        tile_lists = tile_pairs[domain]
        live_tiles = tile_count[domain]

        def block_step(running, first_tile):
            cells_near = lax.dynamic_slice_in_dim(tile_lists[0], first_tile, tile_block)
            cells_far = lax.dynamic_slice_in_dim(tile_lists[1], first_tile, tile_block)
            live_mask = ((first_tile + jnp.arange(tile_block, dtype=jnp.int32)) < live_tiles).astype(jnp.float32)
            near_cells = own_cells[:, :, cells_near]
            far_cells = extended[:, :, cells_far]
            strength = pair_table[own_types[cells_near][:, :, None], wide_types[cells_far][:, None, :]].astype(jnp.float32)
            strength = strength * live_mask[:, None, None]
            delta_x = near_cells[:, 0, :, :, None] - far_cells[:, 0, :, None, :]
            delta_y = near_cells[:, 1, :, :, None] - far_cells[:, 1, :, None, :]
            delta_z = near_cells[:, 2, :, :, None] - far_cells[:, 2, :, None, :]
            distance = delta_x * delta_x + delta_y * delta_y + delta_z * delta_z
            weight = strength * jnp.exp(-distance * inverse_width) * pair_scale
            pair_force = jnp.stack([jnp.sum(weight * delta_x, axis=3), jnp.sum(weight * delta_y, axis=3), jnp.sum(weight * delta_z, axis=3)], axis=1)
            return running.at[:, :, cells_near].add(pair_force), None

        starts = jnp.arange(0, TILES, tile_block, dtype=jnp.int32)
        return lax.scan(block_step, jnp.zeros((NBEADS, 3, CELLS, CAP), jnp.float32), starts)[0]

    per_domain = lax.map(domain_forces, domain_ids)
    forces = jnp.transpose(per_domain, (1, 2, 0, 3, 4)).reshape(NBEADS, 3, ATOMS)
    momenta_out = momenta_moved + inner_step * forces
    return positions_out, momenta_out, thermo_out, forces, types_out
```

```python
import functools
import math

import jax
import jax.numpy as jnp
import numpy as np
from jax import lax
from jax.experimental import pallas as pl
from jax.experimental.pallas import tpu as pltpu
from jax.sharding import PartitionSpec as P

NBEADS = 16
CAP = 128
CHAIN = 4
NTYPES = 128
outer_step = 0.2
inner_step = 0.05
thermal = 1.0
chain_mass = 2.0
cycle_freq = 2.0
pair_reach = 0.4
offsets = (1, -1, 2, -2)
opposite = (1, 0, 3, 2)
MESH = pl.DeviceIdType.MESH
f32 = jnp.float32
bf16 = jnp.bfloat16

reach2 = pair_reach * pair_reach
spread = math.sqrt(1.0 / (reach2 * math.log(2.0)))
log_scale = math.log2(1.0 / (reach2 * NBEADS))
centre = (0.5, 4.0, 3.0)
batch = 8
prep_unroll = 8
halo_parts = 4


def split3(x):
    a = x.astype(bf16).astype(f32)
    b = (x - a).astype(bf16).astype(f32)
    return a, b, x - a - b


def cycle_map(peers):
    k = np.arange(NBEADS)
    w = 2.0 * cycle_freq * np.sin(math.pi * k / NBEADS)
    r = outer_step * w
    c = np.cos(r)
    s = np.where(k > 0, np.sin(r) / np.where(k > 0, w, 1.0), outer_step)
    b = -w * np.sin(r)
    lag = (k[:, None] - k[None, :]) % NBEADS
    phase = np.cos(2.0 * math.pi / NBEADS * (lag[:, :, None] * k % NBEADS))
    mc, ms, mb = ((phase * v).sum(2) / NBEADS for v in (c, s, b))
    maps = [[mc, ms], [mb, mc]]
    per = NBEADS // peers
    size = peers * 8
    big = np.zeros((3 * size, 3 * size))

    def place(p, kind, bead, comp, half):
        row = (kind * per + bead) * 3 + comp
        if row < 8:
            return half * size + p * 8 + row
        return 2 * size + p * 8 + half * 4 + row - 8

    for half in range(2):
        for comp in range(3):
            for kind in range(2):
                for kind2 in range(2):
                    for j in range(NBEADS):
                        for i in range(NBEADS):
                            to = place(j // per, kind, j % per, comp, half)
                            fro = place(i // per, kind2, i % per, comp, half)
                            big[to, fro] = maps[kind][kind2][j, i]
    return big.astype(np.float32)


def front_kernel(
    peers, domains,
    pos, mom, thermo, types, masses, rows, count, bigm,
    ext, momo, tho,
    send1, recv1, send2, recv2, pd, pth, mass, mask, inverse, into, gat, sca,
    e_out, e_in, l_out, l_in,
    s1, r1, s2, r2, se, re, sl, rl, sh, rh,
):
    slots = pos.shape[2]
    chunk = slots // peers
    half = chunk // 2
    me_b = lax.axis_index("bead")
    me_s = lax.axis_index("space")

    def ring(off):
        return lax.rem(me_b + off + peers, peers)

    def domain(off):
        return lax.rem(me_s + off + domains, domains)

    def lanes(start, size, unit=128):
        return pl.ds(pl.multiple_of(start, unit), size)

    barrier = pltpu.get_barrier_semaphore()
    for off in range(1, peers):
        pl.semaphore_signal(barrier, inc=1, device_id=(ring(off), me_s), device_id_type=MESH)
    for off in offsets:
        pl.semaphore_signal(barrier, inc=1, device_id=(me_b, domain(off)), device_id_type=MESH)

    m1, m2, m3 = split3(masses[...])
    mass_rows = jnp.concatenate([m1, m2, m3, jnp.zeros((5, NTYPES), f32)], axis=0).astype(bf16)
    kind_iota = lax.broadcasted_iota(jnp.int32, (NTYPES, chunk), 0)

    def find_mass(n, carry):
        at = lanes(n * chunk, chunk)
        kind = jnp.broadcast_to(types[:, at], (NTYPES, chunk))
        onehot = jnp.where(kind == kind_iota, 1.0, 0.0).astype(bf16)
        got = jnp.dot(mass_rows, onehot, preferred_element_type=f32)
        found = got[0:1] + got[1:2] + got[2:3]
        mass[:, at] = found
        inverse[:, at] = 1.0 / found
        return carry

    lax.fori_loop(0, peers, find_mass, 0)
    pl.semaphore_wait(barrier, peers - 1 + len(offsets))

    def chain(p):
        at = lanes(p * chunk, chunk)
        inv = inverse[:, at]
        h = 0.5 * outer_step
        vel = []
        for bead in range(2):
            z = [thermo[bead, link, :, at] for link in range(CHAIN)]
            q = mom[bead, :, at]
            old = [q * q * inv * (1.0 / chain_mass)] + [v * v for v in z[:-1]]
            z[3] = z[3] + h * (old[3] - thermal / chain_mass)
            for link in (2, 1, 0):
                drive = old[link] - thermal / chain_mass
                z[link] = z[link] * jnp.exp(z[link + 1] * -h) + h * drive
            for link in range(CHAIN):
                first = (bead * CHAIN + link) * 3
                pth[first : first + 3, at] = z[link]
            vel.append(q * jnp.exp(z[0] * -h) * inv)
        send1[p, 0:3, 0:chunk] = pos[0, :, at]
        send1[p, 3:6, 0:chunk] = pos[1, :, at]
        send1[p, 6:8, 0:chunk] = vel[0][0:2]
        for part in range(2):
            cut = slice(part * half, (part + 1) * half)
            to = slice(chunk, chunk + half)
            send1[p, 4 * part : 4 * part + 1, to] = vel[0][2:3, cut]
            send1[p, 4 * part + 1 : 4 * part + 4, to] = vel[1][:, cut]

    def exchange(out, got, ssem, rsem, off):
        p = ring(off)
        return pltpu.make_async_remote_copy(
            src_ref=out.at[p], dst_ref=got.at[me_b], send_sem=ssem.at[off], recv_sem=rsem.at[off],
            device_id=(p, me_s), device_id_type=MESH)

    def arrival(out, got, ssem, rsem, off):
        p = ring(-off)
        return pltpu.make_async_remote_copy(
            src_ref=out.at[p], dst_ref=got.at[p], send_sem=ssem.at[off], recv_sem=rsem.at[off],
            device_id=(p, me_s), device_id_type=MESH)

    def far_first(step):
        k = (step + 1) // 2
        return peers // 2 + jnp.where(lax.rem(step, 2) == 1, -k, k)

    def send_chunk(step, carry):
        off = far_first(step)
        chain(ring(off))
        exchange(send1, recv1, s1, r1, off).start()
        return carry

    lax.fori_loop(0, peers - 1, send_chunk, 0)
    chain(me_b)
    recv1[me_b] = send1[me_b]

    into[...] = jnp.full(into.shape, -1.0, f32)
    into[0:4, 0 : rows.shape[1]] = rows[...].astype(f32)
    listed = into[0:4]
    place = lax.broadcasted_iota(jnp.int32, (1, CAP), 1)
    for c in range(4):
        other = opposite[c]
        live = place < count[0, other]
        into[8 + c : 9 + c] = jnp.where(live, listed[other : other + 1], -1.0)
    landing = into[...].T

    def leave_map(n, carry):
        at = lanes(n * CAP, CAP)
        slot = (lax.broadcasted_iota(jnp.int32, (CAP, CAP), 0) + n * CAP).astype(f32)
        for c in range(4):
            gat[at, c * CAP : (c + 1) * CAP] = jnp.where(slot == listed[c : c + 1], 1.0, 0.0).astype(bf16)
        return carry

    lax.fori_loop(0, slots // CAP, leave_map, 0, unroll=2)

    pth[24:32] = jnp.zeros((8, slots), f32)
    pth[24:25] = types[...].astype(f32)

    def early_gather(n, total):
        at = lanes(n * chunk, chunk)
        x1, x2, x3 = split3(pth[0:24, at])
        left = jnp.concatenate([x1, x2, x3, pth[24:32, at]], axis=0).astype(bf16)
        return total + jnp.dot(left, gat[at, :], preferred_element_type=f32)

    got = lax.fori_loop(0, peers, early_gather, jnp.zeros((80, 4 * CAP), f32))
    early = got[0:24] + got[24:48] + got[48:72]

    def hop(out, got, ssem, rsem, c, to):
        return pltpu.make_async_remote_copy(
            src_ref=out.at[c], dst_ref=got.at[c], send_sem=ssem.at[c], recv_sem=rsem.at[c],
            device_id=(me_b, domain(to)), device_id_type=MESH)

    for c in range(4):
        e_out[c, 0:24] = early[:, c * CAP : (c + 1) * CAP]
        e_out[c, 24:32] = got[72:80, c * CAP : (c + 1) * CAP]
        hop(e_out, e_in, se, re, c, offsets[c]).start()

    def land_map(n, carry):
        at = lanes(n * CAP, CAP)
        slot = (lax.broadcasted_iota(jnp.int32, (CAP, CAP), 1) + n * CAP).astype(f32)
        for c in range(4):
            sca[c * CAP : (c + 1) * CAP, at] = jnp.where(slot == landing[:, 8 + c : 9 + c], 1.0, 0.0).astype(bf16)
        return carry

    lax.fori_loop(0, slots // CAP, land_map, 0, unroll=2)

    def take1(off, carry):
        arrival(send1, recv1, s1, r1, off).wait_recv()
        return carry

    lax.fori_loop(1, peers, take1, 0)
    size = peers * 8
    right = jnp.concatenate(
        [recv1[:, :, n * half : (n + 1) * half].reshape(size, half) for n in range(3)], axis=0)
    mixed = jnp.dot(bigm[...], right, preferred_element_type=f32, precision=lax.Precision.HIGHEST)
    for n in range(3):
        send2[:, :, n * half : (n + 1) * half] = mixed[n * size : (n + 1) * size].reshape(peers, 8, half)

    def send_mixed(step, carry):
        exchange(send2, recv2, s2, r2, far_first(step)).start()
        return carry

    lax.fori_loop(0, peers - 1, send_mixed, 0)
    recv2[me_b] = send2[me_b]

    for c in range(4):
        hop(e_out, e_in, se, re, c, -offsets[c]).wait_recv()
    x1, x2, x3 = split3(jnp.concatenate([e_in[c, 0:24] for c in range(4)], axis=1))
    kinds = jnp.concatenate([e_in[c, 24:32] for c in range(4)], axis=1)
    tag = lax.broadcasted_iota(jnp.int32, (8, 4 * CAP), 0)
    kinds = jnp.where(tag == 0, kinds, 1.0)
    early_left = jnp.concatenate([x1, x2, x3, kinds], axis=0).astype(bf16)

    def early_land(n, carry):
        at = lanes(n * 256, 256)
        new = jnp.dot(early_left, sca[:, at], preferred_element_type=f32)
        hit = new[73:74]
        mask[:, at] = hit
        merged = jnp.where(hit > 0.5, new[0:24] + new[24:48] + new[48:72], pth[0:24, at])
        for bead in range(2):
            for link in range(CHAIN):
                first = (bead * CHAIN + link) * 3
                tho[bead, link, :, at] = merged[first : first + 3]
        ext[1, 6:7, at] = jnp.where(hit > 0.5, new[72:73], pth[24:25, at])
        return carry

    ext[1, 7:8] = jnp.zeros((1, slots), f32)
    lax.fori_loop(0, slots // 256, early_land, 0, unroll=2)

    row_id = lax.broadcasted_iota(jnp.int32, (8, chunk), 0)

    def unpack(p, total):
        at = lanes(p * chunk, chunk)
        m = mass[:, at]
        main = recv2[p, :, 0:chunk]
        rest = recv2[p, :, chunk : chunk + half]
        top = jnp.where(row_id < 6, main, main * m)
        low = jnp.concatenate([rest[0:4] * m[:, 0:half], rest[4:8] * m[:, half:chunk]], axis=1)
        both = jnp.concatenate([top, low, jnp.zeros((4, chunk), f32)], axis=0)
        pd[:, at] = both
        left = jnp.concatenate(split3(both), axis=0).astype(bf16)
        return total + jnp.dot(left, gat[at, :], preferred_element_type=f32)

    total = unpack(me_b, jnp.zeros((48, 4 * CAP), f32))

    def take2(step, total):
        off = far_first(peers - 2 - step)
        arrival(send2, recv2, s2, r2, off).wait_recv()
        return unpack(ring(-off), total)

    total = lax.fori_loop(0, peers - 1, take2, total)
    late = total[0:16] + total[16:32] + total[32:48]
    late_row = lax.broadcasted_iota(jnp.int32, (16, CAP), 0)
    is_x = (late_row == 0) | (late_row == 3)
    for c in range(4):
        block = late[:, c * CAP : (c + 1) * CAP]
        l_out[c] = jnp.where(is_x, block - float(offsets[c]), block)
        hop(l_out, l_in, sl, rl, c, offsets[c]).start()

    for c in range(4):
        hop(l_out, l_in, sl, rl, c, -offsets[c]).wait_recv()
    late_left = jnp.concatenate(
        split3(jnp.concatenate([l_in[c] for c in range(4)], axis=1)), axis=0).astype(bf16)

    def late_land(n, carry):
        at = lanes(n * 256, 256)
        new = jnp.dot(late_left, sca[:, at], preferred_element_type=f32)
        merged = jnp.where(mask[:, at] > 0.5, new[0:16] + new[16:32] + new[32:48], pd[:, at])
        ext[1, 0:6, at] = merged[0:6]
        momo[0, :, at] = merged[6:9]
        momo[1, :, at] = merged[9:12]
        return carry

    width = slots // halo_parts

    def halo(side, part, to):
        cut = slice(part * width, (part + 1) * width)
        return pltpu.make_async_remote_copy(
            src_ref=ext.at[1, :, cut], dst_ref=ext.at[2 * side, :, cut],
            send_sem=sh.at[side, part], recv_sem=rh.at[side, part],
            device_id=(me_b, domain(to)), device_id_type=MESH)

    blocks = width // 256
    for part in range(halo_parts):
        lax.fori_loop(part * blocks, (part + 1) * blocks, late_land, 0, unroll=2)
        halo(0, part, 1).start()
        halo(1, part, -1).start()

    for part in range(halo_parts):
        halo(0, part, -1).wait_recv()
        halo(1, part, 1).wait_recv()

    def drain(off, carry):
        exchange(send1, recv1, s1, r1, off).wait_send()
        exchange(send2, recv2, s2, r2, off).wait_send()
        return carry

    lax.fori_loop(1, peers, drain, 0)
    for c in range(4):
        hop(e_out, e_in, se, re, c, offsets[c]).wait_send()
        hop(l_out, l_in, sl, rl, c, offsets[c]).wait_send()
    for part in range(halo_parts):
        halo(0, part, 1).wait_send()
        halo(1, part, -1).wait_send()


def front(peers, domains, pos, mom, thermo, types, masses, rows, count, bigm):
    slots = pos.shape[2]
    chunk = slots // peers
    packed = chunk + chunk // 2
    vm = pl.BlockSpec(memory_space=pltpu.VMEM)
    sm = pl.BlockSpec(memory_space=pltpu.SMEM)
    dma = pltpu.SemaphoreType.DMA
    shape = jax.ShapeDtypeStruct
    return pl.pallas_call(
        functools.partial(front_kernel, peers, domains),
        out_shape=(
            shape((3, 8, slots), f32),
            shape((2, 3, slots), f32),
            shape((2, CHAIN, 3, slots), f32),
        ),
        in_specs=[vm, vm, vm, vm, vm, vm, sm, vm],
        out_specs=(vm, vm, vm),
        scratch_shapes=[
            pltpu.VMEM((peers, 8, packed), f32),
            pltpu.VMEM((peers, 8, packed), f32),
            pltpu.VMEM((peers, 8, packed), f32),
            pltpu.VMEM((peers, 8, packed), f32),
            pltpu.VMEM((16, slots), f32),
            pltpu.VMEM((32, slots), f32),
            pltpu.VMEM((1, slots), f32),
            pltpu.VMEM((1, slots), f32),
            pltpu.VMEM((1, slots), f32),
            pltpu.VMEM((CAP, CAP), f32),
            pltpu.VMEM((slots, 4 * CAP), bf16),
            pltpu.VMEM((4 * CAP, slots), bf16),
            pltpu.VMEM((4, 32, CAP), f32),
            pltpu.VMEM((4, 32, CAP), f32),
            pltpu.VMEM((4, 16, CAP), f32),
            pltpu.VMEM((4, 16, CAP), f32),
            dma((peers,)), dma((peers,)), dma((peers,)), dma((peers,)),
            dma((4,)), dma((4,)), dma((4,)), dma((4,)),
            dma((2, halo_parts)), dma((2, halo_parts)),
        ],
        compiler_params=pltpu.CompilerParams(
            collective_id=0, has_side_effects=True, vmem_limit_bytes=48 * 2**20),
        name="front",
    )(pos, mom, thermo, types, masses, rows, count, bigm)


def force_kernel(
    tiles, count, ext, mom, thermo, table,
    force, momo, poso, kindo, tho,
    far, strength, near, moment, total, w0, w1, sem,
):
    slots = ext.shape[2]
    cells = slots // CAP
    keep = pltpu.make_async_copy(thermo, tho, sem)
    keep.start()
    rid = lax.broadcasted_iota(jnp.int32, (8, CAP), 0)
    comp = lax.rem(rid, 3)
    lane = lax.broadcasted_iota(jnp.int32, (CAP, CAP), 1).astype(f32)
    subl = lax.broadcasted_iota(jnp.int32, (CAP, CAP), 0).astype(f32)

    def cell_at(c):
        return pl.ds(pl.multiple_of(c * CAP, CAP), CAP)

    def scaled(dom, c):
        block = ext[dom, :, cell_at(c)]
        middle = jnp.where(comp == 0, centre[0] - (dom - 1.0), jnp.where(comp == 1, centre[1], centre[2]))
        u = (block - middle) * spread
        sq = u * u * -0.5
        n0 = sq[0:1] + sq[1:2] + sq[2:3]
        n1 = sq[3:4] + sq[4:5] + sq[5:6]
        return block, u, n0, n1, jnp.where(rid < 6, u, jnp.where(rid == 6, n0, n1))

    def prepare_far(dom):
        def body(c, carry):
            block, u, n0, n1, x = scaled(dom, c)
            x1, x2, x3 = split3(x)
            kind = jnp.broadcast_to(block[6:7], (8, CAP))
            rows = jnp.concatenate(
                [x1, x1, x2, x2, x1, x3, jnp.ones_like(x1), kind, jnp.zeros((64, CAP), f32)], axis=0)
            turned = rows.T
            cell = dom * cells + c
            far[cell, :, 128:256] = turned.astype(bf16)
            far[cell, :, 0:128] = jnp.where(turned[:, 56:57] == lane, 1.0, 0.0).astype(bf16)
            one = jnp.ones((1, CAP), f32)
            zero = jnp.zeros((1, CAP), f32)
            q = jnp.concatenate(
                [one, x1[0:3], x2[0:3], zero, one, x1[3:6], x2[3:6], zero], axis=0).astype(bf16)
            moment[cell] = jnp.concatenate([q, q], axis=1)
            return carry

        lax.fori_loop(0, cells, body, 0, unroll=prep_unroll)

    for dom in range(3):
        prepare_far(dom)

    def prepare_near(c, carry):
        block, u, n0, n1, x = scaled(1, c)
        x1, x2, x3 = split3(x)
        kind = jnp.broadcast_to(block[6:7], (CAP, CAP))
        onehot = jnp.where(kind == subl, 1.0, 0.0).astype(bf16)
        strength[c] = jnp.dot(table[...], onehot, preferred_element_type=f32).astype(bf16)
        for bead in range(2):
            mine = (rid >= 3 * bead) & (rid < 3 * bead + 3)
            unit = jnp.where(rid == 6 + bead, 1.0, 0.0)
            m1, m2, m3 = split3((n0 if bead == 0 else n1) + log_scale)
            norms = jnp.where(rid == 0, m1, jnp.where(rid == 1, m2, jnp.where(rid == 2, m3, 0.0)))
            y1, y2, y3 = (jnp.where(mine, v, 0.0) for v in (x1, x2, x3))
            z1 = jnp.where(mine, x1, unit)
            rows = jnp.concatenate([z1, y2, z1, y2, y3, z1, norms, jnp.zeros_like(norms)], axis=0)
            near[c, :, bead * CAP : (bead + 1) * CAP] = rows.astype(bf16)
        return carry

    lax.fori_loop(0, cells, prepare_near, 0, unroll=prep_unroll)
    near[cells] = jnp.zeros(near.shape[1:], bf16)
    strength[cells] = jnp.zeros(strength.shape[1:], bf16)
    total[...] = jnp.zeros(total.shape, f32)
    w1[...] = jnp.zeros(w1.shape, bf16)
    live_tiles = count[0]
    last = tiles.shape[1] - 1

    def weigh(t, w, k):
        at = jnp.minimum(t, last)
        i = jnp.where(t < live_tiles, tiles[0, at], cells)
        j = tiles[1, at]
        s = jnp.dot(far[j, :, 0:128], strength[i], preferred_element_type=f32)
        e = jnp.dot(far[j, :, 128:192], near[i], preferred_element_type=f32)
        for bead in range(2):
            cut = slice(bead * CAP, (bead + 1) * CAP)
            weight = s * jnp.exp2(e[:, cut])
            high = weight.astype(bf16)
            w[k, 0:CAP, cut] = high
            w[k, CAP : 2 * CAP, cut] = (weight - high.astype(f32)).astype(bf16)

    def gather_force(t, w, k):
        at = jnp.clip(t, 0, last)
        i = jnp.where((t >= 0) & (t < live_tiles), tiles[0, at], cells)
        f = jnp.dot(moment[tiles[1, at]], w[k], preferred_element_type=f32)
        total[i, 0] += f[0:8, 0:CAP]
        total[i, 1] += f[8:16, CAP : 2 * CAP]

    def step(b, carry):
        base = b * 2 * batch
        for k in range(batch):
            weigh(base + k, w0, k)
            gather_force(base - batch + k, w1, k)
        for k in range(batch):
            weigh(base + batch + k, w1, k)
            gather_force(base + k, w0, k)
        return carry

    steps = (live_tiles + 2 * batch - 1) // (2 * batch)
    lax.fori_loop(0, steps, step, 0)
    for k in range(batch):
        gather_force(steps * 2 * batch - batch + k, w1, k)

    def finish(c, carry):
        block, u, n0, n1, x = scaled(1, c)
        at = cell_at(c)
        for bead in range(2):
            r = total[c, bead]
            got = (u[3 * bead : 3 * bead + 3] * r[0:1] - r[1:4] - r[4:7]) * (1.0 / spread)
            force[bead, :, at] = got
            momo[bead, :, at] = mom[bead, :, at] + inner_step * got
            poso[bead, :, at] = block[3 * bead : 3 * bead + 3]
        kindo[:, at] = block[6:7].astype(jnp.int32)
        return carry

    lax.fori_loop(0, cells, finish, 0, unroll=prep_unroll)
    keep.wait()


def pair_forces(tiles, count, ext, mom, thermo, table):
    slots = ext.shape[2]
    cells = slots // CAP
    vm = pl.BlockSpec(memory_space=pltpu.VMEM)
    sm = pl.BlockSpec(memory_space=pltpu.SMEM)
    hbm = pl.BlockSpec(memory_space=pl.ANY)
    shape = jax.ShapeDtypeStruct
    beads = shape((2, 3, slots), f32)
    return pl.pallas_call(
        force_kernel,
        out_shape=(beads, beads, beads, shape((1, slots), jnp.int32), shape(thermo.shape, f32)),
        in_specs=[sm, sm, vm, vm, hbm, vm],
        out_specs=(vm, vm, vm, vm, hbm),
        scratch_shapes=[
            pltpu.VMEM((3 * cells, CAP, 256), bf16),
            pltpu.VMEM((cells + 1, CAP, CAP), bf16),
            pltpu.VMEM((cells + 1, 64, 256), bf16),
            pltpu.VMEM((3 * cells, 16, 256), bf16),
            pltpu.VMEM((cells + 1, 2, 8, CAP), f32),
            pltpu.VMEM((batch, 256, 256), bf16),
            pltpu.VMEM((batch, 256, 256), bf16),
            pltpu.SemaphoreType.DMA,
        ],
        compiler_params=pltpu.CompilerParams(vmem_limit_bytes=48 * 2**20),
        name="pair_forces",
    )(tiles, count, ext, mom, thermo, table)


def per_device(peers, domains, positions, momenta, thermostat, atom_types, masses, pair_table,
               tile_pairs, tile_count, move_rows, move_count):
    slots = positions.shape[2]
    ext, moved, thermo = front(
        peers, domains, positions, momenta, thermostat, atom_types.reshape(1, slots),
        masses.reshape(1, -1), move_rows[0], move_count, jnp.asarray(cycle_map(peers)))
    forces, momenta_out, positions_out, kinds, thermo_out = pair_forces(
        tile_pairs[0], tile_count, ext, moved, thermo, pair_table)
    return positions_out, momenta_out, thermo_out, forces, kinds.reshape(slots)


def solution(mesh):
    placed = (
        P("bead", None, "space"),
        P("bead", None, "space"),
        P("bead", None, None, "space"),
        P("space"),
        P(),
        P(),
        P("space", None, None),
        P("space"),
        P("space", None, None),
        P("space", None),
    )
    return jax.shard_map(
        functools.partial(per_device, mesh.shape["bead"], mesh.shape["space"]),
        mesh=mesh,
        in_specs=placed,
        out_specs=(
            P("bead", None, "space"),
            P("bead", None, "space"),
            P("bead", None, None, "space"),
            P("bead", None, "space"),
            P("space"),
        ),
        check_vma=False,
    )
```

```python
import functools
import math

import jax
import jax.numpy as jnp
import numpy as np
from jax import lax
from jax.experimental import pallas as pl
from jax.experimental.pallas import tpu as pltpu
from jax.sharding import PartitionSpec as P

NBEADS = 16
CAP = 128
CHAIN = 4
NTYPES = 128
outer_step = 0.2
inner_step = 0.05
thermal = 1.0
chain_mass = 2.0
cycle_freq = 2.0
pair_reach = 0.4
offsets = (1, -1, 2, -2)
opposite = (1, 0, 3, 2)
MESH = pl.DeviceIdType.MESH
f32 = jnp.float32
bf16 = jnp.bfloat16

reach2 = pair_reach * pair_reach
spread = math.sqrt(1.0 / (reach2 * math.log(2.0)))
log_scale = math.log2(1.0 / (reach2 * NBEADS))
centre = (0.5, 4.0, 3.0)
batch = 16
prep_unroll = 16
halo_parts = 4


def split3(x):
    a = x.astype(bf16).astype(f32)
    b = (x - a).astype(bf16).astype(f32)
    return a, b, x - a - b


def cycle_map(peers):
    k = np.arange(NBEADS)
    w = 2.0 * cycle_freq * np.sin(math.pi * k / NBEADS)
    r = outer_step * w
    c = np.cos(r)
    s = np.where(k > 0, np.sin(r) / np.where(k > 0, w, 1.0), outer_step)
    b = -w * np.sin(r)
    lag = (k[:, None] - k[None, :]) % NBEADS
    phase = np.cos(2.0 * math.pi / NBEADS * (lag[:, :, None] * k % NBEADS))
    mc, ms, mb = ((phase * v).sum(2) / NBEADS for v in (c, s, b))
    maps = [[mc, ms], [mb, mc]]
    per = NBEADS // peers
    size = peers * 8
    big = np.zeros((3 * size, 3 * size))

    def place(p, kind, bead, comp, half):
        row = (kind * 3 + comp) * per + bead
        if row < 8:
            return half * size + p * 8 + row
        return 2 * size + p * 8 + half * 4 + row - 8

    for half in range(2):
        for comp in range(3):
            for kind in range(2):
                for kind2 in range(2):
                    for j in range(NBEADS):
                        for i in range(NBEADS):
                            to = place(j // per, kind, j % per, comp, half)
                            fro = place(i // per, kind2, i % per, comp, half)
                            big[to, fro] = maps[kind][kind2][j, i]
    return big.astype(np.float32)


def front_kernel(
    peers, domains,
    pos, mom, thermo, types, masses, rows, count, bigm,
    ext, momo, tho,
    send1, recv1, send2, recv2, pd, pth, mass, mask, inverse, into, gat, sca,
    e_out, e_in, l_out, l_in,
    s1, r1, s2, r2, se, re, sl, rl, sh, rh,
):
    slots = pos.shape[2]
    chunk = slots // peers
    half = chunk // 2
    me_b = lax.axis_index("bead")
    me_s = lax.axis_index("space")

    def ring(off):
        return lax.rem(me_b + off + peers, peers)

    def domain(off):
        return lax.rem(me_s + off + domains, domains)

    def lanes(start, size, unit=128):
        return pl.ds(pl.multiple_of(start, unit), size)

    barrier = pltpu.get_barrier_semaphore()
    for off in range(1, peers):
        pl.semaphore_signal(barrier, inc=1, device_id=(ring(off), me_s), device_id_type=MESH)
    for off in offsets:
        pl.semaphore_signal(barrier, inc=1, device_id=(me_b, domain(off)), device_id_type=MESH)

    m1, m2, m3 = split3(masses[...])
    mass_rows = jnp.concatenate([m1, m2, m3, jnp.zeros((5, NTYPES), f32)], axis=0).astype(bf16)
    kind_iota = lax.broadcasted_iota(jnp.int32, (NTYPES, chunk), 0)

    def find_mass(n, carry):
        at = lanes(n * chunk, chunk)
        kind = jnp.broadcast_to(types[:, at], (NTYPES, chunk))
        onehot = jnp.where(kind == kind_iota, 1.0, 0.0).astype(bf16)
        got = jnp.dot(mass_rows, onehot, preferred_element_type=f32)
        found = got[0:1] + got[1:2] + got[2:3]
        mass[:, at] = found
        inverse[:, at] = 1.0 / found
        return carry

    lax.fori_loop(0, peers, find_mass, 0)
    pl.semaphore_wait(barrier, peers - 1 + len(offsets))

    def chain(p):
        at = lanes(p * chunk, chunk)
        inv = inverse[:, at]
        h = 0.5 * outer_step
        q = jnp.concatenate([mom[n, :, at] for n in range(3)], axis=0)
        z = [
            jnp.concatenate([thermo[b, n, link : link + 1, at] for n in range(3) for b in range(2)], axis=0)
            for link in range(CHAIN)
        ]
        old = [q * q * inv * (1.0 / chain_mass)] + [v * v for v in z[:-1]]
        z[3] = z[3] + h * (old[3] - thermal / chain_mass)
        for link in (2, 1, 0):
            drive = old[link] - thermal / chain_mass
            z[link] = z[link] * jnp.exp(z[link + 1] * -h) + h * drive
        for link in range(CHAIN):
            pth[6 * link : 6 * link + 6, at] = z[link]
        vel = q * jnp.exp(z[0] * -h) * inv
        for n in range(3):
            send1[p, 2 * n : 2 * n + 2, 0:chunk] = pos[n, :, at]
        send1[p, 6:8, 0:chunk] = vel[0:2]
        for part in range(2):
            send1[p, 4 * part : 4 * part + 4, chunk : chunk + half] = vel[2:6, part * half : (part + 1) * half]

    def exchange(out, got, ssem, rsem, off):
        p = ring(off)
        return pltpu.make_async_remote_copy(
            src_ref=out.at[p], dst_ref=got.at[me_b], send_sem=ssem.at[off], recv_sem=rsem.at[off],
            device_id=(p, me_s), device_id_type=MESH)

    def arrival(out, got, ssem, rsem, off):
        p = ring(-off)
        return pltpu.make_async_remote_copy(
            src_ref=out.at[p], dst_ref=got.at[p], send_sem=ssem.at[off], recv_sem=rsem.at[off],
            device_id=(p, me_s), device_id_type=MESH)

    def far_first(step):
        k = (step + 1) // 2
        return peers // 2 + jnp.where(lax.rem(step, 2) == 1, -k, k)

    def send_chunk(step, carry):
        off = far_first(step)
        chain(ring(off))
        exchange(send1, recv1, s1, r1, off).start()
        return carry

    lax.fori_loop(0, peers - 1, send_chunk, 0)
    chain(me_b)
    recv1[me_b] = send1[me_b]

    into[...] = jnp.full(into.shape, -1.0, f32)
    into[0:4, 0 : rows.shape[1]] = rows[...].astype(f32)
    listed = into[0:4]
    place = lax.broadcasted_iota(jnp.int32, (1, CAP), 1)
    for c in range(4):
        other = opposite[c]
        live = place < count[0, other]
        into[8 + c : 9 + c] = jnp.where(live, listed[other : other + 1], -1.0)
    landing = into[...].T

    def leave_map(n, carry):
        at = lanes(n * CAP, CAP)
        slot = (lax.broadcasted_iota(jnp.int32, (CAP, CAP), 0) + n * CAP).astype(f32)
        for c in range(4):
            gat[at, c * CAP : (c + 1) * CAP] = jnp.where(slot == listed[c : c + 1], 1.0, 0.0).astype(bf16)
        return carry

    lax.fori_loop(0, slots // CAP, leave_map, 0, unroll=2)

    pth[24:32] = jnp.zeros((8, slots), f32)
    pth[24:25] = types[...].astype(f32)

    def early_gather(n, total):
        at = lanes(n * chunk, chunk)
        x1, x2, x3 = split3(pth[0:24, at])
        left = jnp.concatenate([x1, x2, x3, pth[24:32, at]], axis=0).astype(bf16)
        return total + jnp.dot(left, gat[at, :], preferred_element_type=f32)

    got = lax.fori_loop(0, peers, early_gather, jnp.zeros((80, 4 * CAP), f32))
    early = got[0:24] + got[24:48] + got[48:72]

    def hop(out, got, ssem, rsem, c, to):
        return pltpu.make_async_remote_copy(
            src_ref=out.at[c], dst_ref=got.at[c], send_sem=ssem.at[c], recv_sem=rsem.at[c],
            device_id=(me_b, domain(to)), device_id_type=MESH)

    for c in range(4):
        e_out[c, 0:24] = early[:, c * CAP : (c + 1) * CAP]
        e_out[c, 24:32] = got[72:80, c * CAP : (c + 1) * CAP]
        hop(e_out, e_in, se, re, c, offsets[c]).start()

    def land_map(n, carry):
        at = lanes(n * CAP, CAP)
        slot = (lax.broadcasted_iota(jnp.int32, (CAP, CAP), 1) + n * CAP).astype(f32)
        for c in range(4):
            sca[c * CAP : (c + 1) * CAP, at] = jnp.where(slot == landing[:, 8 + c : 9 + c], 1.0, 0.0).astype(bf16)
        return carry

    lax.fori_loop(0, slots // CAP, land_map, 0, unroll=2)

    def take1(off, carry):
        arrival(send1, recv1, s1, r1, off).wait_recv()
        return carry

    lax.fori_loop(1, peers, take1, 0)
    size = peers * 8
    right = jnp.concatenate(
        [recv1[:, :, n * half : (n + 1) * half].reshape(size, half) for n in range(3)], axis=0)
    mixed = jnp.dot(bigm[...], right, preferred_element_type=f32, precision=lax.Precision.HIGHEST)
    for n in range(3):
        send2[:, :, n * half : (n + 1) * half] = mixed[n * size : (n + 1) * size].reshape(peers, 8, half)

    def send_mixed(step, carry):
        exchange(send2, recv2, s2, r2, far_first(step)).start()
        return carry

    lax.fori_loop(0, peers - 1, send_mixed, 0)
    recv2[me_b] = send2[me_b]

    for c in range(4):
        hop(e_out, e_in, se, re, c, -offsets[c]).wait_recv()
    x1, x2, x3 = split3(jnp.concatenate([e_in[c, 0:24] for c in range(4)], axis=1))
    kinds = jnp.concatenate([e_in[c, 24:32] for c in range(4)], axis=1)
    tag = lax.broadcasted_iota(jnp.int32, (8, 4 * CAP), 0)
    kinds = jnp.where(tag == 0, kinds, 1.0)
    early_left = jnp.concatenate([x1, x2, x3, kinds], axis=0).astype(bf16)

    def early_land(n, carry):
        at = lanes(n * 256, 256)
        new = jnp.dot(early_left, sca[:, at], preferred_element_type=f32)
        hit = new[73:74]
        mask[:, at] = hit
        merged = jnp.where(hit > 0.5, new[0:24] + new[24:48] + new[48:72], pth[0:24, at])
        for bead in range(2):
            for n in range(3):
                for link in range(CHAIN):
                    first = 6 * link + 2 * n + bead
                    tho[bead, n, link : link + 1, at] = merged[first : first + 1]
        ext[1, 6:7, at] = jnp.where(hit > 0.5, new[72:73], pth[24:25, at])
        return carry

    ext[1, 7:8] = jnp.zeros((1, slots), f32)
    lax.fori_loop(0, slots // 256, early_land, 0, unroll=2)

    row_id = lax.broadcasted_iota(jnp.int32, (8, chunk), 0)

    def unpack(p, total):
        at = lanes(p * chunk, chunk)
        m = mass[:, at]
        main = recv2[p, :, 0:chunk]
        rest = recv2[p, :, chunk : chunk + half]
        top = jnp.where(row_id < 6, main, main * m)
        low = jnp.concatenate([rest[0:4] * m[:, 0:half], rest[4:8] * m[:, half:chunk]], axis=1)
        both = jnp.concatenate([top, low, jnp.zeros((4, chunk), f32)], axis=0)
        pd[:, at] = both
        left = jnp.concatenate(split3(both), axis=0).astype(bf16)
        return total + jnp.dot(left, gat[at, :], preferred_element_type=f32)

    total = unpack(me_b, jnp.zeros((48, 4 * CAP), f32))

    def take2(step, total):
        off = far_first(peers - 2 - step)
        arrival(send2, recv2, s2, r2, off).wait_recv()
        return unpack(ring(-off), total)

    total = lax.fori_loop(0, peers - 1, take2, total)
    late = total[0:16] + total[16:32] + total[32:48]
    late_row = lax.broadcasted_iota(jnp.int32, (16, CAP), 0)
    is_x = late_row < 2
    for c in range(4):
        block = late[:, c * CAP : (c + 1) * CAP]
        l_out[c] = jnp.where(is_x, block - float(offsets[c]), block)
        hop(l_out, l_in, sl, rl, c, offsets[c]).start()

    for c in range(4):
        hop(l_out, l_in, sl, rl, c, -offsets[c]).wait_recv()
    late_left = jnp.concatenate(
        split3(jnp.concatenate([l_in[c] for c in range(4)], axis=1)), axis=0).astype(bf16)

    def late_land(n, carry):
        at = lanes(n * 256, 256)
        new = jnp.dot(late_left, sca[:, at], preferred_element_type=f32)
        merged = jnp.where(mask[:, at] > 0.5, new[0:16] + new[16:32] + new[32:48], pd[:, at])
        ext[1, 0:6, at] = merged[0:6]
        for n in range(3):
            momo[n, :, at] = merged[6 + 2 * n : 8 + 2 * n]
        return carry

    width = slots // halo_parts

    def halo(side, part, to):
        cut = slice(part * width, (part + 1) * width)
        return pltpu.make_async_remote_copy(
            src_ref=ext.at[1, :, cut], dst_ref=ext.at[2 * side, :, cut],
            send_sem=sh.at[side, part], recv_sem=rh.at[side, part],
            device_id=(me_b, domain(to)), device_id_type=MESH)

    blocks = width // 256
    for part in range(halo_parts):
        lax.fori_loop(part * blocks, (part + 1) * blocks, late_land, 0, unroll=2)
        halo(0, part, 1).start()
        halo(1, part, -1).start()

    for part in range(halo_parts):
        halo(0, part, -1).wait_recv()
        halo(1, part, 1).wait_recv()

    def drain(off, carry):
        exchange(send1, recv1, s1, r1, off).wait_send()
        exchange(send2, recv2, s2, r2, off).wait_send()
        return carry

    lax.fori_loop(1, peers, drain, 0)
    for c in range(4):
        hop(e_out, e_in, se, re, c, offsets[c]).wait_send()
        hop(l_out, l_in, sl, rl, c, offsets[c]).wait_send()
    for part in range(halo_parts):
        halo(0, part, 1).wait_send()
        halo(1, part, -1).wait_send()


def front(peers, domains, pos, mom, thermo, types, masses, rows, count, bigm):
    slots = pos.shape[2]
    chunk = slots // peers
    packed = chunk + chunk // 2
    vm = pl.BlockSpec(memory_space=pltpu.VMEM)
    sm = pl.BlockSpec(memory_space=pltpu.SMEM)
    dma = pltpu.SemaphoreType.DMA
    shape = jax.ShapeDtypeStruct
    return pl.pallas_call(
        functools.partial(front_kernel, peers, domains),
        out_shape=(
            shape((3, 8, slots), f32),
            shape((3, 2, slots), f32),
            shape((2, 3, CHAIN, slots), f32),
        ),
        in_specs=[vm, vm, vm, vm, vm, vm, sm, vm],
        out_specs=(vm, vm, vm),
        scratch_shapes=[
            pltpu.VMEM((peers, 8, packed), f32),
            pltpu.VMEM((peers, 8, packed), f32),
            pltpu.VMEM((peers, 8, packed), f32),
            pltpu.VMEM((peers, 8, packed), f32),
            pltpu.VMEM((16, slots), f32),
            pltpu.VMEM((32, slots), f32),
            pltpu.VMEM((1, slots), f32),
            pltpu.VMEM((1, slots), f32),
            pltpu.VMEM((1, slots), f32),
            pltpu.VMEM((CAP, CAP), f32),
            pltpu.VMEM((slots, 4 * CAP), bf16),
            pltpu.VMEM((4 * CAP, slots), bf16),
            pltpu.VMEM((4, 32, CAP), f32),
            pltpu.VMEM((4, 32, CAP), f32),
            pltpu.VMEM((4, 16, CAP), f32),
            pltpu.VMEM((4, 16, CAP), f32),
            dma((peers,)), dma((peers,)), dma((peers,)), dma((peers,)),
            dma((4,)), dma((4,)), dma((4,)), dma((4,)),
            dma((2, halo_parts)), dma((2, halo_parts)),
        ],
        compiler_params=pltpu.CompilerParams(
            collective_id=0, has_side_effects=True, vmem_limit_bytes=48 * 2**20),
        name="front",
    )(pos, mom, thermo, types, masses, rows, count, bigm)


def force_kernel(
    tiles, count, ext, mom, thermo, table,
    force, momo, poso, kindo, tho,
    far, near, strength, moment, total, w0, w1, sem,
):
    slots = ext.shape[2]
    cells = slots // CAP
    keep = pltpu.make_async_copy(thermo, tho, sem)
    keep.start()
    rid = lax.broadcasted_iota(jnp.int32, (8, CAP), 0)
    comp = rid // 2
    parity = lax.rem(rid, 2)
    subl = lax.broadcasted_iota(jnp.int32, (CAP, CAP), 0).astype(f32)

    def cell_at(c):
        return pl.ds(pl.multiple_of(c * CAP, CAP), CAP)

    def scaled(dom, c, extra):
        block = ext[dom, :, cell_at(c)]
        middle = jnp.where(comp == 0, centre[0] - (dom - 1.0), jnp.where(comp == 1, centre[1], centre[2]))
        u = (block - middle) * spread
        sq = u * u * -0.5
        n = sq[0:2] + sq[2:4] + sq[4:6] + extra
        return block, jnp.concatenate([u[0:6], n], axis=0)

    def prepare_far(dom):
        def body(c, carry):
            block, x = scaled(dom, c, 0.0)
            x1, x2, x3 = split3(x)
            z1 = jnp.where(rid < 6, x1, 1.0)
            z2 = jnp.where(rid < 6, x2, 1.0)
            cell = dom * cells + c
            kind = jnp.broadcast_to(block[6:7], (CAP, CAP))
            rows = jnp.concatenate([x1, x2, x3, z1, z2, z1, jnp.zeros((80, CAP), f32)], axis=0)
            far[cell, :, 0:CAP] = jnp.where(kind == subl, 1.0, 0.0).astype(bf16).T
            far[cell, :, CAP : 2 * CAP] = rows.astype(bf16).T
            q = jnp.concatenate([z1, jnp.where(rid < 6, x2, 0.0)], axis=0).astype(bf16)
            moment[cell, :, 0:CAP] = q
            moment[cell, :, CAP : 2 * CAP] = q
            return carry

        lax.fori_loop(0, cells, body, 0, unroll=prep_unroll)

    for dom in range(3):
        prepare_far(dom)

    def prepare_near(c, carry):
        block, x = scaled(1, c, log_scale)
        x1, x2, x3 = split3(x)
        kind = jnp.broadcast_to(block[6:7], (CAP, CAP))
        onehot = jnp.where(kind == subl, 1.0, 0.0).astype(bf16)
        strength[c] = jnp.dot(table[...], onehot, preferred_element_type=f32).astype(bf16)
        for bead in range(2):
            mine = (rid < 6) & (parity == bead)
            norm = rid == 6 + bead
            y1 = jnp.where(mine, x1, jnp.where(norm, 1.0, 0.0))
            y12 = jnp.where(mine, x2, jnp.where(norm, x1, 0.0))
            y2 = jnp.where(mine | norm, x2, 0.0)
            y3 = jnp.where(mine | norm, x3, 0.0)
            near[c, :, bead * CAP : (bead + 1) * CAP] = jnp.concatenate([y1, y1, y1, y12, y2, y3], axis=0).astype(bf16)
        return carry

    lax.fori_loop(0, cells, prepare_near, 0, unroll=prep_unroll)
    near[cells] = jnp.zeros(near.shape[1:], bf16)
    strength[cells] = jnp.zeros(strength.shape[1:], bf16)
    total[...] = jnp.zeros(total.shape, f32)
    w1[...] = jnp.zeros(w1.shape, bf16)
    live_tiles = count[0]
    last = tiles.shape[1] - 1
    even = parity == 0

    def weigh(t, w, k):
        at = jnp.minimum(t, last)
        i = jnp.where(t < live_tiles, tiles[0, at], cells)
        j = tiles[1, at]
        s = jnp.dot(far[j, :, 0:CAP], strength[i], preferred_element_type=f32)
        e = jnp.dot(far[j, :, CAP : CAP + 48], near[i], preferred_element_type=f32)
        for bead in range(2):
            cut = slice(bead * CAP, (bead + 1) * CAP)
            weight = s * jnp.exp2(e[:, cut])
            high = weight.astype(bf16)
            w[k, 0:CAP, cut] = high
            w[k, CAP : 2 * CAP, cut] = (weight - high.astype(f32)).astype(bf16)

    def gather_force(t, w, k):
        at = jnp.clip(t, 0, last)
        i = jnp.where((t >= 0) & (t < live_tiles), tiles[0, at], cells)
        f = jnp.dot(moment[tiles[1, at]], w[k], preferred_element_type=f32)
        f = f[0:8] + f[8:16]
        total[i] += jnp.where(even, f[:, 0:CAP], f[:, CAP : 2 * CAP])

    def step(b, carry):
        base = b * 2 * batch
        for k in range(batch):
            weigh(base + k, w0, k)
            gather_force(base - batch + k, w1, k)
        for k in range(batch):
            weigh(base + batch + k, w1, k)
            gather_force(base + k, w0, k)
        return carry

    steps = (live_tiles + 2 * batch - 1) // (2 * batch)
    lax.fori_loop(0, steps, step, 0)
    for k in range(batch):
        gather_force(steps * 2 * batch - batch + k, w1, k)

    def finish(c, carry):
        block, x = scaled(1, c, 0.0)
        at = cell_at(c)
        r = total[c]
        got = (x * jnp.where(even, r[6:7], r[7:8]) - r) * (1.0 / spread)
        for n in range(3):
            pair = got[2 * n : 2 * n + 2]
            force[n, :, at] = pair
            momo[n, :, at] = mom[n, :, at] + inner_step * pair
            poso[n, :, at] = block[2 * n : 2 * n + 2]
        kindo[:, at] = block[6:7].astype(jnp.int32)
        return carry

    lax.fori_loop(0, cells, finish, 0, unroll=prep_unroll)
    keep.wait()


def pair_forces(tiles, count, ext, mom, thermo, table):
    slots = ext.shape[2]
    cells = slots // CAP
    vm = pl.BlockSpec(memory_space=pltpu.VMEM)
    sm = pl.BlockSpec(memory_space=pltpu.SMEM)
    hbm = pl.BlockSpec(memory_space=pl.ANY)
    shape = jax.ShapeDtypeStruct
    beads = shape((3, 2, slots), f32)
    return pl.pallas_call(
        force_kernel,
        out_shape=(beads, beads, beads, shape((1, slots), jnp.int32), shape(thermo.shape, f32)),
        in_specs=[sm, sm, vm, vm, hbm, vm],
        out_specs=(vm, vm, vm, vm, hbm),
        scratch_shapes=[
            pltpu.VMEM((3 * cells, CAP, 256), bf16),
            pltpu.VMEM((cells + 1, 48, 256), bf16),
            pltpu.VMEM((cells + 1, CAP, CAP), bf16),
            pltpu.VMEM((3 * cells, 16, 256), bf16),
            pltpu.VMEM((cells + 1, 8, CAP), f32),
            pltpu.VMEM((batch, 256, 256), bf16),
            pltpu.VMEM((batch, 256, 256), bf16),
            pltpu.SemaphoreType.DMA,
        ],
        compiler_params=pltpu.CompilerParams(vmem_limit_bytes=48 * 2**20),
        name="pair_forces",
    )(tiles, count, ext, mom, thermo, table)


def per_device(peers, domains, positions, momenta, thermostat, atom_types, masses, pair_table,
               tile_pairs, tile_count, move_rows, move_count):
    slots = positions.shape[2]
    ext, moved, thermo = front(
        peers, domains, positions.transpose(1, 0, 2), momenta.transpose(1, 0, 2),
        thermostat.transpose(0, 2, 1, 3), atom_types.reshape(1, slots),
        masses.reshape(1, -1), move_rows[0], move_count, jnp.asarray(cycle_map(peers)))
    forces, momenta_out, positions_out, kinds, thermo_out = pair_forces(
        tile_pairs[0], tile_count, ext, moved, thermo, pair_table)
    return (
        positions_out.transpose(1, 0, 2), momenta_out.transpose(1, 0, 2),
        thermo_out.transpose(0, 2, 1, 3), forces.transpose(1, 0, 2), kinds.reshape(slots))


def solution(mesh):
    placed = (
        P("bead", None, "space"),
        P("bead", None, "space"),
        P("bead", None, None, "space"),
        P("space"),
        P(),
        P(),
        P("space", None, None),
        P("space"),
        P("space", None, None),
        P("space", None),
    )
    return jax.shard_map(
        functools.partial(per_device, mesh.shape["bead"], mesh.shape["space"]),
        mesh=mesh,
        in_specs=placed,
        out_specs=(
            P("bead", None, "space"),
            P("bead", None, "space"),
            P("bead", None, None, "space"),
            P("bead", None, "space"),
            P("space"),
        ),
        check_vma=False,
    )
```

```python
import functools
import math

import jax
import jax.numpy as jnp
import numpy as np
from jax import lax
from jax.experimental import pallas as pl
from jax.experimental.pallas import tpu as pltpu
from jax.sharding import PartitionSpec as P

NBEADS = 16
CAP = 128
CHAIN = 4
NTYPES = 128
outer_step = 0.2
inner_step = 0.05
thermal = 1.0
chain_mass = 2.0
cycle_freq = 2.0
pair_reach = 0.4
offsets = (1, -1, 2, -2)
opposite = (1, 0, 3, 2)
MESH = pl.DeviceIdType.MESH
f32 = jnp.float32
bf16 = jnp.bfloat16

reach2 = pair_reach * pair_reach
spread = math.sqrt(1.0 / (reach2 * math.log(2.0)))
log_scale = math.log2(1.0 / (reach2 * NBEADS))
centre = (0.5, 4.0, 3.0)
batch = 16
prep_unroll = 16


def split3(x):
    a = x.astype(bf16).astype(f32)
    b = (x - a).astype(bf16).astype(f32)
    return a, b, x - a - b


def cycle_map(peers):
    k = np.arange(NBEADS)
    w = 2.0 * cycle_freq * np.sin(math.pi * k / NBEADS)
    r = outer_step * w
    c = np.cos(r)
    s = np.where(k > 0, np.sin(r) / np.where(k > 0, w, 1.0), outer_step)
    b = -w * np.sin(r)
    lag = (k[:, None] - k[None, :]) % NBEADS
    phase = np.cos(2.0 * math.pi / NBEADS * (lag[:, :, None] * k % NBEADS))
    mc, ms, mb = ((phase * v).sum(2) / NBEADS for v in (c, s, b))
    maps = [[mc, ms], [mb, mc]]
    per = NBEADS // peers
    size = peers * 8
    big = np.zeros((3 * size, 3 * size))

    def place(p, kind, bead, comp, half):
        row = (kind * 3 + comp) * per + bead
        if row < 8:
            return half * size + p * 8 + row
        return 2 * size + p * 8 + half * 4 + row - 8

    for half in range(2):
        for comp in range(3):
            for kind in range(2):
                for kind2 in range(2):
                    for j in range(NBEADS):
                        for i in range(NBEADS):
                            to = place(j // per, kind, j % per, comp, half)
                            fro = place(i // per, kind2, i % per, comp, half)
                            big[to, fro] = maps[kind][kind2][j, i]
    small = np.zeros((3, size, size))
    for n, m in enumerate((mc, mb, ms)):
        for comp in range(3):
            for j in range(NBEADS):
                for i in range(NBEADS):
                    to = j // per * 8 + comp * per + j % per
                    small[n, to, i // per * 8 + comp * per + i % per] = m[j, i]
    return big.astype(np.float32), small.reshape(3 * size, size).astype(np.float32)


def front_kernel(
    peers, domains,
    pos_in, mom_in, thermo_in, types_in, masses_in, rows_in, count_in, big_in, small_in,
    ext, momo, tho,
    pos, mom, thermo, types, masses, rows, count, bigm, smallm,
    send1, recv1, send2, recv2, pth, mass, mask, into, picked, gat, sca,
    mig1, got1, mig2, got2, scale, e_out, e_in,
    load, s1, r1, s2, r2, sm1, rm1, sm2, rm2, se, re, sh, rh,
):
    slots = pos.shape[2]
    chunk = slots // peers
    half = chunk // 2
    me_b = lax.axis_index("bead")
    me_s = lax.axis_index("space")

    def ring(off):
        return lax.rem(me_b + off + peers, peers)

    def domain(off):
        return lax.rem(me_s + off + domains, domains)

    def lanes(start, size):
        return pl.ds(pl.multiple_of(start, CAP), size)

    def class_offset(c):
        return (1 + c // 2) * (1 - 2 * (c % 2))

    pairs = [
        (types_in, types), (masses_in, masses), (pos_in, pos), (mom_in, mom), (thermo_in, thermo),
        (rows_in, rows), (count_in, count), (big_in, bigm), (small_in, smallm)]
    loads = [pltpu.make_async_copy(src, dst, load.at[n]) for n, (src, dst) in enumerate(pairs)]
    for copy in loads:
        copy.start()

    barrier = pltpu.get_barrier_semaphore()
    for off in range(1, peers):
        pl.semaphore_signal(barrier, inc=1, device_id=(ring(off), me_s), device_id_type=MESH)
    for off in offsets:
        pl.semaphore_signal(barrier, inc=1, device_id=(me_b, domain(off)), device_id_type=MESH)

    for q in range(peers):
        @pl.when(me_b != q)
        def _():
            pl.semaphore_signal(
                barrier, inc=1, device_id=(q, domain(-class_offset(q // 2))), device_id_type=MESH)

    for copy in loads[0:5]:
        copy.wait()
    m1, m2, m3 = split3(masses[...])
    mass_rows = jnp.concatenate([m1, m2, m3, jnp.zeros((5, NTYPES), f32)], axis=0).astype(bf16)
    kind_iota = lax.broadcasted_iota(jnp.int32, (NTYPES, chunk), 0)

    def chain(p):
        at = lanes(p * chunk, chunk)
        kind = types[:, at]
        onehot = jnp.where(jnp.broadcast_to(kind, (NTYPES, chunk)) == kind_iota, 1.0, 0.0).astype(bf16)
        found = jnp.dot(mass_rows, onehot, preferred_element_type=f32)
        found = found[0:1] + found[1:2] + found[2:3]
        mass[:, at] = found
        inv = 1.0 / found
        h = 0.5 * outer_step
        place = jnp.concatenate([pos[n, :, at] for n in range(3)], axis=0)
        q = jnp.concatenate([mom[n, :, at] for n in range(3)], axis=0)
        z = [
            jnp.concatenate([thermo[b, n, link : link + 1, at] for n in range(3) for b in range(2)], axis=0)
            for link in range(CHAIN)
        ]
        old = [q * q * inv * (1.0 / chain_mass)] + [v * v for v in z[:-1]]
        z[3] = z[3] + h * (old[3] - thermal / chain_mass)
        for link in (2, 1, 0):
            drive = old[link] - thermal / chain_mass
            z[link] = z[link] * jnp.exp(z[link + 1] * -h) + h * drive
        for link in range(CHAIN):
            pth[6 * link : 6 * link + 6, at] = z[link]
        vel = q * jnp.exp(z[0] * -h) * inv
        none = jnp.zeros((2, chunk), f32)
        pth[24:32, at] = jnp.concatenate([kind.astype(f32), found, none, none, none], axis=0)
        pth[32:40, at] = jnp.concatenate([place, none], axis=0)
        pth[40:48, at] = jnp.concatenate([vel, none], axis=0)
        send1[p, 0:6, 0:chunk] = place
        send1[p, 6:8, 0:chunk] = vel[0:2]
        for part in range(2):
            send1[p, 4 * part : 4 * part + 4, chunk : chunk + half] = vel[2:6, part * half : (part + 1) * half]

    def exchange(out, got, ssem, rsem, off):
        p = ring(off)
        return pltpu.make_async_remote_copy(
            src_ref=out.at[p], dst_ref=got.at[me_b], send_sem=ssem.at[off], recv_sem=rsem.at[off],
            device_id=(p, me_s), device_id_type=MESH)

    def arrival(out, got, ssem, rsem, off):
        p = ring(-off)
        return pltpu.make_async_remote_copy(
            src_ref=out.at[p], dst_ref=got.at[p], send_sem=ssem.at[off], recv_sem=rsem.at[off],
            device_id=(p, me_s), device_id_type=MESH)

    def far_first(step):
        k = (step + 1) // 2
        return peers // 2 + jnp.where(lax.rem(step, 2) == 1, -k, k)

    first = ring(far_first(0))
    chain(first)
    pl.semaphore_wait(barrier, 2 * (peers - 1) + len(offsets))
    exchange(send1, recv1, s1, r1, far_first(0)).start()

    def send_chunk(step, carry):
        off = far_first(step)
        chain(ring(off))
        exchange(send1, recv1, s1, r1, off).start()
        return carry

    lax.fori_loop(1, peers - 1, send_chunk, 0)
    chain(me_b)
    recv1[me_b] = send1[me_b]

    for copy in loads[5:]:
        copy.wait()
    into[...] = jnp.full(into.shape, -1.0, f32)
    into[0:4, 0 : rows.shape[1]] = rows[...].astype(f32)
    listed = into[0:4]
    spot = lax.broadcasted_iota(jnp.int32, (1, CAP), 1)
    for c in range(4):
        other = opposite[c]
        live = spot < jnp.broadcast_to(count[:, other : other + 1], (1, CAP))
        into[8 + c : 9 + c] = jnp.where(live, listed[other : other + 1], -1.0)
    landing = into[...].T
    picked[...] = jnp.zeros(picked.shape, f32)
    row_iota = lax.broadcasted_iota(jnp.int32, (CAP, CAP), 0)

    def pick(n, carry):
        for k in range(chunk // CAP):
            slot = (row_iota + (n * chunk + k * CAP)).astype(f32)
            for c in range(4):
                gat[k * CAP : (k + 1) * CAP, c * CAP : (c + 1) * CAP] = jnp.where(
                    slot == listed[c : c + 1], 1.0, 0.0).astype(bf16)
        left = jnp.concatenate(split3(pth[:, lanes(n * chunk, chunk)]), axis=0).astype(bf16)
        picked[...] += jnp.dot(left, gat[...], preferred_element_type=f32)
        return carry

    lax.fori_loop(0, peers, pick, 0)
    leaving = picked[0:48] + picked[48:96] + picked[96:144]
    low = lax.broadcasted_iota(jnp.int32, (8, CAP), 1) < CAP // 2

    def swap(x):
        return pltpu.roll(x, CAP // 2, 1)

    for c in range(4):
        cut = slice(c * CAP, (c + 1) * CAP)
        place, vel = leaving[32:40, cut], leaving[40:48, cut]
        mig1[2 * c] = jnp.where(low, place, swap(vel))
        mig1[2 * c + 1] = jnp.where(low, swap(place), vel)
        m = jnp.broadcast_to(leaving[25:26, cut], (8, CAP))
        scale[2 * c] = jnp.where(low, 1.0, swap(m))
        scale[2 * c + 1] = jnp.where(low, 1.0, m)

    def send_leaving(step, carry):
        exchange(mig1, got1, sm1, rm1, far_first(step)).start()
        return carry

    lax.fori_loop(0, peers - 1, send_leaving, 0)
    got1[me_b] = mig1[me_b]

    def hop(out, got, ssem, rsem, c, to):
        return pltpu.make_async_remote_copy(
            src_ref=out.at[c], dst_ref=got.at[c], send_sem=ssem.at[c], recv_sem=rsem.at[c],
            device_id=(me_b, domain(to)), device_id_type=MESH)

    for c in range(4):
        e_out[c] = leaving[0:32, c * CAP : (c + 1) * CAP]
        hop(e_out, e_in, se, re, c, offsets[c]).start()

    def land_map(n, carry):
        at = lanes(n * CAP, CAP)
        slot = (lax.broadcasted_iota(jnp.int32, (CAP, CAP), 1) + n * CAP).astype(f32)
        for c in range(4):
            sca[c * CAP : (c + 1) * CAP, at] = jnp.where(slot == landing[:, 8 + c : 9 + c], 1.0, 0.0).astype(bf16)
        return carry

    lax.fori_loop(0, slots // CAP, land_map, 0, unroll=2)

    def take1(off, carry):
        arrival(send1, recv1, s1, r1, off).wait_recv()
        return carry

    lax.fori_loop(1, peers, take1, 0)
    size = peers * 8
    right = jnp.concatenate(
        [recv1[:, :, n * half : (n + 1) * half].reshape(size, half) for n in range(3)], axis=0)
    mixed = jnp.dot(bigm[...], right, preferred_element_type=f32, precision=lax.Precision.HIGHEST)
    for n in range(3):
        send2[:, :, n * half : (n + 1) * half] = mixed[n * size : (n + 1) * size].reshape(peers, 8, half)

    def take_leaving(off, carry):
        arrival(mig1, got1, sm1, rm1, off).wait_recv()
        return carry

    lax.fori_loop(1, peers, take_leaving, 0)
    turned = jnp.dot(
        smallm[...], got1[...].reshape(size, CAP), preferred_element_type=f32,
        precision=lax.Precision.HIGHEST)
    low_all = lax.broadcasted_iota(jnp.int32, (size, CAP), 1) < CAP // 2
    cross = swap(jnp.where(low_all, turned[size : 2 * size], turned[2 * size : 3 * size]))
    mine = class_offset(me_b // 2)
    is_x = (lax.broadcasted_iota(jnp.int32, (8, CAP), 0) < 2) & low
    shift = jnp.where(is_x, mine.astype(f32), 0.0)
    mig2[...] = (turned[0:size] + cross).reshape(peers, 8, CAP) * scale[me_b][None] - shift[None]

    def deliver(p):
        return pltpu.make_async_remote_copy(
            src_ref=mig2.at[p], dst_ref=got2.at[me_b], send_sem=sm2.at[p], recv_sem=rm2.at[me_b],
            device_id=(p, domain(mine)), device_id_type=MESH)

    def delivered(q):
        return pltpu.make_async_remote_copy(
            src_ref=mig2.at[q], dst_ref=got2.at[q], send_sem=sm2.at[q], recv_sem=rm2.at[q],
            device_id=(q, domain(-mine)), device_id_type=MESH)

    def send_turned(p, carry):
        deliver(p).start()
        return carry

    def send_mixed(step, carry):
        exchange(send2, recv2, s2, r2, far_first(step)).start()
        return carry

    lax.fori_loop(0, peers, send_turned, 0)
    lax.fori_loop(0, peers - 1, send_mixed, 0)
    recv2[me_b] = send2[me_b]

    for c in range(4):
        hop(e_out, e_in, se, re, c, -offsets[c]).wait_recv()
    x1, x2, x3 = split3(jnp.concatenate([e_in[c, 0:24] for c in range(4)], axis=1))
    kinds = jnp.concatenate([e_in[c, 24:32] for c in range(4)], axis=1)
    tag = lax.broadcasted_iota(jnp.int32, (8, 4 * CAP), 0)
    kinds = jnp.where(tag == 0, kinds, 1.0)
    early_left = jnp.concatenate([x1, x2, x3, kinds], axis=0).astype(bf16)

    def early_land(n, carry):
        at = lanes(n * 256, 256)
        new = jnp.dot(early_left, sca[:, at], preferred_element_type=f32)
        hit = new[73:74]
        mask[:, at] = hit
        merged = jnp.where(hit > 0.5, new[0:24] + new[24:48] + new[48:72], pth[0:24, at])
        for bead in range(2):
            for n in range(3):
                for link in range(CHAIN):
                    row = 6 * link + 2 * n + bead
                    tho[bead, n, link : link + 1, at] = merged[row : row + 1]
        ext[1, 6:7, at] = jnp.where(hit > 0.5, new[72:73], pth[24:25, at])
        return carry

    ext[1, 7:8] = jnp.zeros((1, slots), f32)
    lax.fori_loop(0, slots // 256, early_land, 0, unroll=2)

    def take_turned(q, carry):
        delivered(q).wait_recv()
        return carry

    lax.fori_loop(0, peers, take_turned, 0)
    came = [(got2[2 * c], got2[2 * c + 1]) for c in range(4)]
    place = jnp.concatenate([jnp.where(low, even, swap(odd)) for even, odd in came], axis=1)
    drift = jnp.concatenate([jnp.where(low, swap(even), odd) for even, odd in came], axis=1)
    late_left = jnp.concatenate(
        split3(jnp.concatenate([place, drift], axis=0)), axis=0).astype(bf16)

    def halo(side, p, to):
        cut = lanes(p * chunk, chunk)
        return pltpu.make_async_remote_copy(
            src_ref=ext.at[1, :, cut], dst_ref=ext.at[2 * side, :, cut],
            send_sem=sh.at[side, p], recv_sem=rh.at[side, p],
            device_id=(me_b, domain(to)), device_id_type=MESH)

    def merge(p):
        at = lanes(p * chunk, chunk)
        new = jnp.dot(late_left, sca[:, at], preferred_element_type=f32)
        new = new[0:16] + new[16:32] + new[32:48]
        hit = mask[:, at] > 0.5
        m = mass[:, at]
        main = recv2[p, :, 0:chunk]
        rest = recv2[p, :, chunk : chunk + half]
        ext[1, 0:6, at] = jnp.where(hit, new[0:6], main[0:6])
        halo(0, p, 1).start()
        halo(1, p, -1).start()
        drift = jnp.concatenate([main[6:8], jnp.concatenate([rest[0:4], rest[4:8]], axis=1)], axis=0)
        drift = jnp.where(hit, new[8:14], drift * m)
        for n in range(3):
            momo[n, :, at] = drift[2 * n : 2 * n + 2]

    merge(me_b)

    def take2(step, carry):
        off = far_first(peers - 2 - step)
        arrival(send2, recv2, s2, r2, off).wait_recv()
        merge(ring(-off))
        return carry

    lax.fori_loop(0, peers - 1, take2, 0)

    def drain(off, carry):
        exchange(send1, recv1, s1, r1, off).wait_send()
        exchange(send2, recv2, s2, r2, off).wait_send()
        exchange(mig1, got1, sm1, rm1, off).wait_send()
        return carry

    lax.fori_loop(1, peers, drain, 0)
    for c in range(4):
        hop(e_out, e_in, se, re, c, offsets[c]).wait_send()

    def take_halo(p, carry):
        deliver(p).wait_send()
        halo(0, p, 1).wait_send()
        halo(1, p, -1).wait_send()
        halo(0, p, -1).wait_recv()
        halo(1, p, 1).wait_recv()
        return carry

    lax.fori_loop(0, peers, take_halo, 0)


def front(peers, domains, pos, mom, thermo, types, masses, rows, count):
    slots = pos.shape[2]
    chunk = slots // peers
    packed = chunk + chunk // 2
    bigm, smallm = (jnp.asarray(m) for m in cycle_map(peers))
    args = (pos, mom, thermo, types, masses, rows, count, bigm, smallm)
    vm = pl.BlockSpec(memory_space=pltpu.VMEM)
    hbm = pl.BlockSpec(memory_space=pltpu.HBM)
    dma = pltpu.SemaphoreType.DMA
    shape = jax.ShapeDtypeStruct
    block = pltpu.VMEM((peers, 8, packed), f32)
    small = pltpu.VMEM((peers, 8, CAP), f32)
    return pl.pallas_call(
        functools.partial(front_kernel, peers, domains),
        out_shape=(
            shape((3, 8, slots), f32),
            shape((3, 2, slots), f32),
            shape((2, 3, CHAIN, slots), f32),
        ),
        in_specs=[hbm] * len(args),
        out_specs=(vm, vm, vm),
        scratch_shapes=[
            *(pltpu.VMEM(a.shape, a.dtype) for a in args),
            block, block, block, block,
            pltpu.VMEM((48, slots), f32),
            pltpu.VMEM((1, slots), f32),
            pltpu.VMEM((1, slots), f32),
            pltpu.VMEM((CAP, CAP), f32),
            pltpu.VMEM((144, 4 * CAP), f32),
            pltpu.VMEM((chunk, 4 * CAP), bf16),
            pltpu.VMEM((4 * CAP, slots), bf16),
            small, small, small, small, small,
            pltpu.VMEM((4, 32, CAP), f32),
            pltpu.VMEM((4, 32, CAP), f32),
            dma((len(args),)),
            *(dma((peers,)) for _ in range(8)),
            dma((4,)), dma((4,)),
            dma((2, peers)), dma((2, peers)),
        ],
        compiler_params=pltpu.CompilerParams(
            collective_id=0, has_side_effects=True, vmem_limit_bytes=48 * 2**20),
        name="front",
    )(*args)


def force_kernel(
    tiles, count, ext, mom, thermo, table,
    force, momo, poso, kindo, tho,
    far, near, strength, moment, total, w0, w1, sem,
):
    slots = ext.shape[2]
    cells = slots // CAP
    keep = pltpu.make_async_copy(thermo, tho, sem)
    keep.start()
    rid = lax.broadcasted_iota(jnp.int32, (8, CAP), 0)
    comp = rid // 2
    parity = lax.rem(rid, 2)
    subl = lax.broadcasted_iota(jnp.int32, (CAP, CAP), 0).astype(f32)

    def cell_at(c):
        return pl.ds(pl.multiple_of(c * CAP, CAP), CAP)

    def scaled(dom, c, extra):
        block = ext[dom, :, cell_at(c)]
        middle = jnp.where(comp == 0, centre[0] - (dom - 1.0), jnp.where(comp == 1, centre[1], centre[2]))
        u = (block - middle) * spread
        sq = u * u * -0.5
        n = sq[0:2] + sq[2:4] + sq[4:6] + extra
        return block, jnp.concatenate([u[0:6], n], axis=0)

    def prepare_far(dom):
        def body(c, carry):
            block, x = scaled(dom, c, 0.0)
            x1, x2, x3 = split3(x)
            z1 = jnp.where(rid < 6, x1, 1.0)
            z2 = jnp.where(rid < 6, x2, 1.0)
            cell = dom * cells + c
            kind = jnp.broadcast_to(block[6:7], (CAP, CAP))
            rows = jnp.concatenate([x1, x2, x3, z1, z2, z1, jnp.zeros((80, CAP), f32)], axis=0)
            far[cell, :, 0:CAP] = jnp.where(kind == subl, 1.0, 0.0).astype(bf16).T
            far[cell, :, CAP : 2 * CAP] = rows.astype(bf16).T
            q = jnp.concatenate([z1, jnp.where(rid < 6, x2, 0.0)], axis=0).astype(bf16)
            moment[cell, :, 0:CAP] = q
            moment[cell, :, CAP : 2 * CAP] = q
            return carry

        lax.fori_loop(0, cells, body, 0, unroll=prep_unroll)

    for dom in range(3):
        prepare_far(dom)

    def prepare_near(c, carry):
        block, x = scaled(1, c, log_scale)
        x1, x2, x3 = split3(x)
        kind = jnp.broadcast_to(block[6:7], (CAP, CAP))
        onehot = jnp.where(kind == subl, 1.0, 0.0).astype(bf16)
        strength[c] = jnp.dot(table[...], onehot, preferred_element_type=f32).astype(bf16)
        for bead in range(2):
            mine = (rid < 6) & (parity == bead)
            norm = rid == 6 + bead
            y1 = jnp.where(mine, x1, jnp.where(norm, 1.0, 0.0))
            y12 = jnp.where(mine, x2, jnp.where(norm, x1, 0.0))
            y2 = jnp.where(mine | norm, x2, 0.0)
            y3 = jnp.where(mine | norm, x3, 0.0)
            near[c, :, bead * CAP : (bead + 1) * CAP] = jnp.concatenate([y1, y1, y1, y12, y2, y3], axis=0).astype(bf16)
        return carry

    lax.fori_loop(0, cells, prepare_near, 0, unroll=prep_unroll)
    near[cells] = jnp.zeros(near.shape[1:], bf16)
    strength[cells] = jnp.zeros(strength.shape[1:], bf16)
    total[...] = jnp.zeros(total.shape, f32)
    w1[...] = jnp.zeros(w1.shape, bf16)
    live_tiles = count[0]
    last = tiles.shape[1] - 1
    even = parity == 0

    def weigh(t, w, k):
        at = jnp.minimum(t, last)
        i = jnp.where(t < live_tiles, tiles[0, at], cells)
        j = tiles[1, at]
        s = jnp.dot(far[j, :, 0:CAP], strength[i], preferred_element_type=f32)
        e = jnp.dot(far[j, :, CAP : CAP + 48], near[i], preferred_element_type=f32)
        for bead in range(2):
            cut = slice(bead * CAP, (bead + 1) * CAP)
            weight = s * jnp.exp2(e[:, cut])
            high = weight.astype(bf16)
            w[k, 0:CAP, cut] = high
            w[k, CAP : 2 * CAP, cut] = (weight - high.astype(f32)).astype(bf16)

    def gather_force(t, w, k):
        at = jnp.clip(t, 0, last)
        i = jnp.where((t >= 0) & (t < live_tiles), tiles[0, at], cells)
        f = jnp.dot(moment[tiles[1, at]], w[k], preferred_element_type=f32)
        f = f[0:8] + f[8:16]
        total[i] += jnp.where(even, f[:, 0:CAP], f[:, CAP : 2 * CAP])

    def step(b, carry):
        base = b * 2 * batch
        for k in range(batch):
            weigh(base + k, w0, k)
            gather_force(base - batch + k, w1, k)
        for k in range(batch):
            weigh(base + batch + k, w1, k)
            gather_force(base + k, w0, k)
        return carry

    steps = (live_tiles + 2 * batch - 1) // (2 * batch)
    lax.fori_loop(0, steps, step, 0)
    for k in range(batch):
        gather_force(steps * 2 * batch - batch + k, w1, k)

    def finish(c, carry):
        block, x = scaled(1, c, 0.0)
        at = cell_at(c)
        r = total[c]
        got = (x * jnp.where(even, r[6:7], r[7:8]) - r) * (1.0 / spread)
        for n in range(3):
            pair = got[2 * n : 2 * n + 2]
            force[n, :, at] = pair
            momo[n, :, at] = mom[n, :, at] + inner_step * pair
            poso[n, :, at] = block[2 * n : 2 * n + 2]
        kindo[:, at] = block[6:7].astype(jnp.int32)
        return carry

    lax.fori_loop(0, cells, finish, 0, unroll=prep_unroll)
    keep.wait()


def pair_forces(tiles, count, ext, mom, thermo, table):
    slots = ext.shape[2]
    cells = slots // CAP
    vm = pl.BlockSpec(memory_space=pltpu.VMEM)
    sm = pl.BlockSpec(memory_space=pltpu.SMEM)
    hbm = pl.BlockSpec(memory_space=pl.ANY)
    shape = jax.ShapeDtypeStruct
    beads = shape((3, 2, slots), f32)
    return pl.pallas_call(
        force_kernel,
        out_shape=(beads, beads, beads, shape((1, slots), jnp.int32), shape(thermo.shape, f32)),
        in_specs=[sm, sm, vm, vm, hbm, vm],
        out_specs=(vm, vm, vm, vm, hbm),
        scratch_shapes=[
            pltpu.VMEM((3 * cells, CAP, 256), bf16),
            pltpu.VMEM((cells + 1, 48, 256), bf16),
            pltpu.VMEM((cells + 1, CAP, CAP), bf16),
            pltpu.VMEM((3 * cells, 16, 256), bf16),
            pltpu.VMEM((cells + 1, 8, CAP), f32),
            pltpu.VMEM((batch, 256, 256), bf16),
            pltpu.VMEM((batch, 256, 256), bf16),
            pltpu.SemaphoreType.DMA,
        ],
        compiler_params=pltpu.CompilerParams(vmem_limit_bytes=48 * 2**20),
        name="pair_forces",
    )(tiles, count, ext, mom, thermo, table)


def per_device(peers, domains, positions, momenta, thermostat, atom_types, masses, pair_table,
               tile_pairs, tile_count, move_rows, move_count):
    slots = positions.shape[2]
    ext, moved, thermo = front(
        peers, domains, positions.transpose(1, 0, 2), momenta.transpose(1, 0, 2),
        thermostat.transpose(0, 2, 1, 3), atom_types.reshape(1, slots),
        masses.reshape(1, -1), move_rows[0], move_count)
    forces, momenta_out, positions_out, kinds, thermo_out = pair_forces(
        tile_pairs[0], tile_count, ext, moved, thermo, pair_table)
    return (
        positions_out.transpose(1, 0, 2), momenta_out.transpose(1, 0, 2),
        thermo_out.transpose(0, 2, 1, 3), forces.transpose(1, 0, 2), kinds.reshape(slots))


def solution(mesh):
    placed = (
        P("bead", None, "space"),
        P("bead", None, "space"),
        P("bead", None, None, "space"),
        P("space"),
        P(),
        P(),
        P("space", None, None),
        P("space"),
        P("space", None, None),
        P("space", None),
    )
    return jax.shard_map(
        functools.partial(per_device, mesh.shape["bead"], mesh.shape["space"]),
        mesh=mesh,
        in_specs=placed,
        out_specs=(
            P("bead", None, "space"),
            P("bead", None, "space"),
            P("bead", None, None, "space"),
            P("bead", None, "space"),
            P("space"),
        ),
        check_vma=False,
    )
```

```python
import functools
import math

import jax
import jax.numpy as jnp
import numpy as np
from jax import lax
from jax.experimental import pallas as pl
from jax.experimental.pallas import tpu as pltpu
from jax.sharding import PartitionSpec as P

NBEADS = 16
CAP = 128
CHAIN = 4
NTYPES = 128
outer_step = 0.2
inner_step = 0.05
thermal = 1.0
chain_mass = 2.0
cycle_freq = 2.0
pair_reach = 0.4
offsets = (1, -1, 2, -2)
opposite = (1, 0, 3, 2)
MESH = pl.DeviceIdType.MESH
f32 = jnp.float32
bf16 = jnp.bfloat16

reach2 = pair_reach * pair_reach
spread = math.sqrt(1.0 / (reach2 * math.log(2.0)))
log_scale = math.log2(1.0 / (reach2 * NBEADS))
centre = (0.5, 4.0, 3.0)
batch = 16
prep_unroll = 16


def split3(x):
    a = x.astype(bf16).astype(f32)
    b = (x - a).astype(bf16).astype(f32)
    return a, b, x - a - b


def cycle_map(peers):
    k = np.arange(NBEADS)
    w = 2.0 * cycle_freq * np.sin(math.pi * k / NBEADS)
    r = outer_step * w
    c = np.cos(r)
    s = np.where(k > 0, np.sin(r) / np.where(k > 0, w, 1.0), outer_step)
    b = -w * np.sin(r)
    lag = (k[:, None] - k[None, :]) % NBEADS
    phase = np.cos(2.0 * math.pi / NBEADS * (lag[:, :, None] * k % NBEADS))
    mc, ms, mb = ((phase * v).sum(2) / NBEADS for v in (c, s, b))
    maps = [[mc, ms], [mb, mc]]
    per = NBEADS // peers
    size = peers * 8
    big = np.zeros((3 * size, 3 * size))

    def place(p, kind, bead, comp, half):
        row = (kind * 3 + comp) * per + bead
        if row < 8:
            return half * size + p * 8 + row
        return 2 * size + p * 8 + half * 4 + row - 8

    for half in range(2):
        for comp in range(3):
            for kind in range(2):
                for kind2 in range(2):
                    for j in range(NBEADS):
                        for i in range(NBEADS):
                            to = place(j // per, kind, j % per, comp, half)
                            fro = place(i // per, kind2, i % per, comp, half)
                            big[to, fro] = maps[kind][kind2][j, i]
    small = np.zeros((3, size, size))
    for n, m in enumerate((mc, mb, ms)):
        for comp in range(3):
            for j in range(NBEADS):
                for i in range(NBEADS):
                    to = j // per * 8 + comp * per + j % per
                    small[n, to, i // per * 8 + comp * per + i % per] = m[j, i]
    return big.astype(np.float32), small.reshape(3 * size, size).astype(np.float32)


def front_kernel(
    peers, domains,
    pos_in, mom_in, thermo_in, types_in, masses_in, rows_in, count_in, big_in, small_in,
    ext_out, momo_out, tho_out,
    pos, mom, thermo, types, masses, rows, count, bigm, smallm,
    send1, recv1, send2, recv2, pth, mass, mask, into, picked, gat, sca,
    mig1, got1, mig2, got2, scale, e_out, e_in, ext, momo, tho,
    load, save, s1, r1, s2, r2, sm1, rm1, sm2, rm2, se, re, sh, rh,
):
    slots = pos.shape[2]
    chunk = slots // peers
    half = chunk // 2
    me_b = lax.axis_index("bead")
    me_s = lax.axis_index("space")

    def ring(off):
        return lax.rem(me_b + off + peers, peers)

    def domain(off):
        return lax.rem(me_s + off + domains, domains)

    def lanes(start, size):
        return pl.ds(pl.multiple_of(start, CAP), size)

    def class_offset(c):
        return (1 + c // 2) * (1 - 2 * (c % 2))

    pairs = [
        (types_in, types), (masses_in, masses), (pos_in, pos), (mom_in, mom), (thermo_in, thermo),
        (rows_in, rows), (count_in, count), (big_in, bigm), (small_in, smallm)]
    loads = [pltpu.make_async_copy(src, dst, load.at[n]) for n, (src, dst) in enumerate(pairs)]
    for copy in loads:
        copy.start()

    barrier = pltpu.get_barrier_semaphore()
    for off in range(1, peers):
        pl.semaphore_signal(barrier, inc=1, device_id=(ring(off), me_s), device_id_type=MESH)
    for off in offsets:
        pl.semaphore_signal(barrier, inc=1, device_id=(me_b, domain(off)), device_id_type=MESH)

    for q in range(peers):
        @pl.when(me_b != q)
        def _():
            pl.semaphore_signal(
                barrier, inc=1, device_id=(q, domain(-class_offset(q // 2))), device_id_type=MESH)

    for copy in loads[0:5]:
        copy.wait()
    m1, m2, m3 = split3(masses[...])
    mass_rows = jnp.concatenate([m1, m2, m3, jnp.zeros((5, NTYPES), f32)], axis=0).astype(bf16)
    kind_iota = lax.broadcasted_iota(jnp.int32, (NTYPES, chunk), 0)

    def chain(p):
        at = lanes(p * chunk, chunk)
        kind = types[:, at]
        onehot = jnp.where(jnp.broadcast_to(kind, (NTYPES, chunk)) == kind_iota, 1.0, 0.0).astype(bf16)
        found = jnp.dot(mass_rows, onehot, preferred_element_type=f32)
        found = found[0:1] + found[1:2] + found[2:3]
        mass[:, at] = found
        inv = 1.0 / found
        h = 0.5 * outer_step
        place = jnp.concatenate([pos[n, :, at] for n in range(3)], axis=0)
        q = jnp.concatenate([mom[n, :, at] for n in range(3)], axis=0)
        z = [
            jnp.concatenate([thermo[b, n, link : link + 1, at] for n in range(3) for b in range(2)], axis=0)
            for link in range(CHAIN)
        ]
        old = [q * q * inv * (1.0 / chain_mass)] + [v * v for v in z[:-1]]
        z[3] = z[3] + h * (old[3] - thermal / chain_mass)
        for link in (2, 1, 0):
            drive = old[link] - thermal / chain_mass
            z[link] = z[link] * jnp.exp(z[link + 1] * -h) + h * drive
        for link in range(CHAIN):
            pth[6 * link : 6 * link + 6, at] = z[link]
        vel = q * jnp.exp(z[0] * -h) * inv
        none = jnp.zeros((2, chunk), f32)
        pth[24:32, at] = jnp.concatenate([kind.astype(f32), found, none, none, none], axis=0)
        pth[32:40, at] = jnp.concatenate([place, none], axis=0)
        pth[40:48, at] = jnp.concatenate([vel, none], axis=0)
        send1[p, 0:6, 0:chunk] = place
        send1[p, 6:8, 0:chunk] = vel[0:2]
        for part in range(2):
            send1[p, 4 * part : 4 * part + 4, chunk : chunk + half] = vel[2:6, part * half : (part + 1) * half]

    def exchange(out, got, ssem, rsem, off):
        p = ring(off)
        return pltpu.make_async_remote_copy(
            src_ref=out.at[p], dst_ref=got.at[me_b], send_sem=ssem.at[off], recv_sem=rsem.at[off],
            device_id=(p, me_s), device_id_type=MESH)

    def arrival(out, got, ssem, rsem, off):
        p = ring(-off)
        return pltpu.make_async_remote_copy(
            src_ref=out.at[p], dst_ref=got.at[p], send_sem=ssem.at[off], recv_sem=rsem.at[off],
            device_id=(p, me_s), device_id_type=MESH)

    def far_first(step):
        k = (step + 1) // 2
        return peers // 2 + jnp.where(lax.rem(step, 2) == 1, -k, k)

    first = ring(far_first(0))
    chain(first)
    pl.semaphore_wait(barrier, 2 * (peers - 1) + len(offsets))
    exchange(send1, recv1, s1, r1, far_first(0)).start()

    def send_chunk(step, carry):
        off = far_first(step)
        chain(ring(off))
        exchange(send1, recv1, s1, r1, off).start()
        return carry

    lax.fori_loop(1, peers - 1, send_chunk, 0)
    chain(me_b)
    recv1[me_b] = send1[me_b]

    for copy in loads[5:]:
        copy.wait()
    into[...] = jnp.full(into.shape, -1.0, f32)
    into[0:4, 0 : rows.shape[1]] = rows[...].astype(f32)
    listed = into[0:4]
    spot = lax.broadcasted_iota(jnp.int32, (1, CAP), 1)
    for c in range(4):
        other = opposite[c]
        live = spot < jnp.broadcast_to(count[:, other : other + 1], (1, CAP))
        into[8 + c : 9 + c] = jnp.where(live, listed[other : other + 1], -1.0)
    landing = into[...].T
    picked[...] = jnp.zeros(picked.shape, f32)
    row_iota = lax.broadcasted_iota(jnp.int32, (CAP, CAP), 0)

    def pick(n, carry):
        for k in range(chunk // CAP):
            slot = (row_iota + (n * chunk + k * CAP)).astype(f32)
            for c in range(4):
                gat[k * CAP : (k + 1) * CAP, c * CAP : (c + 1) * CAP] = jnp.where(
                    slot == listed[c : c + 1], 1.0, 0.0).astype(bf16)
        left = jnp.concatenate(split3(pth[:, lanes(n * chunk, chunk)]), axis=0).astype(bf16)
        picked[...] += jnp.dot(left, gat[...], preferred_element_type=f32)
        return carry

    lax.fori_loop(0, peers, pick, 0)
    leaving = picked[0:48] + picked[48:96] + picked[96:144]
    low = lax.broadcasted_iota(jnp.int32, (8, CAP), 1) < CAP // 2

    def swap(x):
        return pltpu.roll(x, CAP // 2, 1)

    for c in range(4):
        cut = slice(c * CAP, (c + 1) * CAP)
        place, vel = leaving[32:40, cut], leaving[40:48, cut]
        mig1[2 * c] = jnp.where(low, place, swap(vel))
        mig1[2 * c + 1] = jnp.where(low, swap(place), vel)
        m = jnp.broadcast_to(leaving[25:26, cut], (8, CAP))
        scale[2 * c] = jnp.where(low, 1.0, swap(m))
        scale[2 * c + 1] = jnp.where(low, 1.0, m)

    def send_leaving(step, carry):
        exchange(mig1, got1, sm1, rm1, far_first(step)).start()
        return carry

    lax.fori_loop(0, peers - 1, send_leaving, 0)
    got1[me_b] = mig1[me_b]

    def hop(out, got, ssem, rsem, c, to):
        return pltpu.make_async_remote_copy(
            src_ref=out.at[c], dst_ref=got.at[c], send_sem=ssem.at[c], recv_sem=rsem.at[c],
            device_id=(me_b, domain(to)), device_id_type=MESH)

    for c in range(4):
        e_out[c] = leaving[0:32, c * CAP : (c + 1) * CAP]
        hop(e_out, e_in, se, re, c, offsets[c]).start()

    def land_map(n, carry):
        at = lanes(n * CAP, CAP)
        slot = (lax.broadcasted_iota(jnp.int32, (CAP, CAP), 1) + n * CAP).astype(f32)
        for c in range(4):
            sca[c * CAP : (c + 1) * CAP, at] = jnp.where(slot == landing[:, 8 + c : 9 + c], 1.0, 0.0).astype(bf16)
        return carry

    lax.fori_loop(0, slots // CAP, land_map, 0, unroll=2)

    def take1(off, carry):
        arrival(send1, recv1, s1, r1, off).wait_recv()
        return carry

    lax.fori_loop(1, peers, take1, 0)
    size = peers * 8
    right = jnp.concatenate(
        [recv1[:, :, n * half : (n + 1) * half].reshape(size, half) for n in range(3)], axis=0)
    mixed = jnp.dot(bigm[...], right, preferred_element_type=f32, precision=lax.Precision.HIGHEST)
    for n in range(3):
        send2[:, :, n * half : (n + 1) * half] = mixed[n * size : (n + 1) * size].reshape(peers, 8, half)

    def take_leaving(off, carry):
        arrival(mig1, got1, sm1, rm1, off).wait_recv()
        return carry

    lax.fori_loop(1, peers, take_leaving, 0)
    turned = jnp.dot(
        smallm[...], got1[...].reshape(size, CAP), preferred_element_type=f32,
        precision=lax.Precision.HIGHEST)
    low_all = lax.broadcasted_iota(jnp.int32, (size, CAP), 1) < CAP // 2
    cross = swap(jnp.where(low_all, turned[size : 2 * size], turned[2 * size : 3 * size]))
    mine = class_offset(me_b // 2)
    is_x = (lax.broadcasted_iota(jnp.int32, (8, CAP), 0) < 2) & low
    shift = jnp.where(is_x, mine.astype(f32), 0.0)
    mig2[...] = (turned[0:size] + cross).reshape(peers, 8, CAP) * scale[me_b][None] - shift[None]

    def deliver(p):
        return pltpu.make_async_remote_copy(
            src_ref=mig2.at[p], dst_ref=got2.at[me_b], send_sem=sm2.at[p], recv_sem=rm2.at[me_b],
            device_id=(p, domain(mine)), device_id_type=MESH)

    def delivered(q):
        return pltpu.make_async_remote_copy(
            src_ref=mig2.at[q], dst_ref=got2.at[q], send_sem=sm2.at[q], recv_sem=rm2.at[q],
            device_id=(q, domain(-mine)), device_id_type=MESH)

    def send_turned(p, carry):
        deliver(p).start()
        return carry

    def send_mixed(step, carry):
        exchange(send2, recv2, s2, r2, far_first(step)).start()
        return carry

    lax.fori_loop(0, peers, send_turned, 0)
    lax.fori_loop(0, peers - 1, send_mixed, 0)
    recv2[me_b] = send2[me_b]

    for c in range(4):
        hop(e_out, e_in, se, re, c, -offsets[c]).wait_recv()
    x1, x2, x3 = split3(jnp.concatenate([e_in[c, 0:24] for c in range(4)], axis=1))
    kinds = jnp.concatenate([e_in[c, 24:32] for c in range(4)], axis=1)
    tag = lax.broadcasted_iota(jnp.int32, (8, 4 * CAP), 0)
    kinds = jnp.where(tag == 0, kinds, 1.0)
    early_left = jnp.concatenate([x1, x2, x3, kinds], axis=0).astype(bf16)

    def early_land(n, carry):
        at = lanes(n * 256, 256)
        new = jnp.dot(early_left, sca[:, at], preferred_element_type=f32)
        hit = new[73:74]
        mask[:, at] = hit
        merged = jnp.where(hit > 0.5, new[0:24] + new[24:48] + new[48:72], pth[0:24, at])
        for bead in range(2):
            for n in range(3):
                for link in range(CHAIN):
                    row = 6 * link + 2 * n + bead
                    tho[bead, n, link : link + 1, at] = merged[row : row + 1]
        ext[6:7, at] = jnp.where(hit > 0.5, new[72:73], pth[24:25, at])
        return carry

    ext[7:8] = jnp.zeros((1, slots), f32)
    lax.fori_loop(0, slots // 256, early_land, 0, unroll=2)
    chains = pltpu.make_async_copy(tho, tho_out, load.at[0])
    chains.start()

    def take_turned(q, carry):
        delivered(q).wait_recv()
        return carry

    lax.fori_loop(0, peers, take_turned, 0)
    came = [(got2[2 * c], got2[2 * c + 1]) for c in range(4)]
    place = jnp.concatenate([jnp.where(low, even, swap(odd)) for even, odd in came], axis=1)
    drift = jnp.concatenate([jnp.where(low, swap(even), odd) for even, odd in came], axis=1)
    late_left = jnp.concatenate(
        split3(jnp.concatenate([place, drift], axis=0)), axis=0).astype(bf16)

    def halo(side, p, to):
        cut = lanes(p * chunk, chunk)
        return pltpu.make_async_remote_copy(
            src_ref=ext.at[:, cut], dst_ref=ext_out.at[2 * side, :, cut],
            send_sem=sh.at[side, p], recv_sem=rh.at[side, p],
            device_id=(me_b, domain(to)), device_id_type=MESH)

    def keep(p):
        cut = lanes(p * chunk, chunk)
        return (
            pltpu.make_async_copy(ext.at[:, cut], ext_out.at[1, :, cut], save.at[0, p]),
            pltpu.make_async_copy(momo.at[:, :, cut], momo_out.at[:, :, cut], save.at[1, p]))

    def merge(p):
        at = lanes(p * chunk, chunk)
        new = jnp.dot(late_left, sca[:, at], preferred_element_type=f32)
        new = new[0:16] + new[16:32] + new[32:48]
        hit = mask[:, at] > 0.5
        m = mass[:, at]
        main = recv2[p, :, 0:chunk]
        rest = recv2[p, :, chunk : chunk + half]
        ext[0:6, at] = jnp.where(hit, new[0:6], main[0:6])
        halo(0, p, 1).start()
        halo(1, p, -1).start()
        drift = jnp.concatenate([main[6:8], jnp.concatenate([rest[0:4], rest[4:8]], axis=1)], axis=0)
        drift = jnp.where(hit, new[8:14], drift * m)
        for n in range(3):
            momo[n, :, at] = drift[2 * n : 2 * n + 2]
        for copy in keep(p):
            copy.start()

    merge(me_b)

    def take2(step, carry):
        off = far_first(peers - 2 - step)
        arrival(send2, recv2, s2, r2, off).wait_recv()
        merge(ring(-off))
        return carry

    lax.fori_loop(0, peers - 1, take2, 0)

    def drain(off, carry):
        exchange(send1, recv1, s1, r1, off).wait_send()
        exchange(send2, recv2, s2, r2, off).wait_send()
        exchange(mig1, got1, sm1, rm1, off).wait_send()
        return carry

    lax.fori_loop(1, peers, drain, 0)
    for c in range(4):
        hop(e_out, e_in, se, re, c, offsets[c]).wait_send()

    def take_halo(p, carry):
        deliver(p).wait_send()
        halo(0, p, 1).wait_send()
        halo(1, p, -1).wait_send()
        halo(0, p, -1).wait_recv()
        halo(1, p, 1).wait_recv()
        for copy in keep(p):
            copy.wait()
        return carry

    lax.fori_loop(0, peers, take_halo, 0)
    chains.wait()


def front(peers, domains, pos, mom, thermo, types, masses, rows, count):
    slots = pos.shape[2]
    chunk = slots // peers
    packed = chunk + chunk // 2
    bigm, smallm = (jnp.asarray(m) for m in cycle_map(peers))
    args = (pos, mom, thermo, types, masses, rows, count, bigm, smallm)
    hbm = pl.BlockSpec(memory_space=pltpu.HBM)
    dma = pltpu.SemaphoreType.DMA
    shape = jax.ShapeDtypeStruct
    block = pltpu.VMEM((peers, 8, packed), f32)
    small = pltpu.VMEM((peers, 8, CAP), f32)
    return pl.pallas_call(
        functools.partial(front_kernel, peers, domains),
        out_shape=(
            shape((3, 8, slots), f32),
            shape((3, 2, slots), f32),
            shape((2, 3, CHAIN, slots), f32),
        ),
        in_specs=[hbm] * len(args),
        out_specs=(hbm, hbm, hbm),
        scratch_shapes=[
            *(pltpu.VMEM(a.shape, a.dtype) for a in args),
            block, block, block, block,
            pltpu.VMEM((48, slots), f32),
            pltpu.VMEM((1, slots), f32),
            pltpu.VMEM((1, slots), f32),
            pltpu.VMEM((CAP, CAP), f32),
            pltpu.VMEM((144, 4 * CAP), f32),
            pltpu.VMEM((chunk, 4 * CAP), bf16),
            pltpu.VMEM((4 * CAP, slots), bf16),
            small, small, small, small, small,
            pltpu.VMEM((4, 32, CAP), f32),
            pltpu.VMEM((4, 32, CAP), f32),
            pltpu.VMEM((8, slots), f32),
            pltpu.VMEM((3, 2, slots), f32),
            pltpu.VMEM((2, 3, CHAIN, slots), f32),
            dma((len(args),)), dma((2, peers)),
            *(dma((peers,)) for _ in range(8)),
            dma((4,)), dma((4,)),
            dma((2, peers)), dma((2, peers)),
        ],
        compiler_params=pltpu.CompilerParams(
            collective_id=0, has_side_effects=True, vmem_limit_bytes=56 * 2**20),
        name="front",
    )(*args)


def force_kernel(
    tiles, count, ext_in, mom_in, thermo, table,
    force_out, momo_out, poso_out, kindo_out, tho,
    far, near, strength, moment, total, w0, w1, ext, mom, force, momo, poso, kindo, sem,
):
    slots = ext.shape[2]
    cells = slots // CAP
    take = [pltpu.make_async_copy(ext_in.at[d], ext.at[d], sem.at[d]) for d in (1, 0, 2)]
    take.append(pltpu.make_async_copy(mom_in, mom, sem.at[3]))
    keep = pltpu.make_async_copy(thermo, tho, sem.at[4])
    for copy in take:
        copy.start()
    keep.start()
    give = [
        pltpu.make_async_copy(src, dst, sem.at[5 + n])
        for n, (src, dst) in enumerate(
            [(poso, poso_out), (kindo, kindo_out), (force, force_out), (momo, momo_out)])]
    rid = lax.broadcasted_iota(jnp.int32, (8, CAP), 0)
    comp = rid // 2
    parity = lax.rem(rid, 2)
    subl = lax.broadcasted_iota(jnp.int32, (CAP, CAP), 0).astype(f32)

    def cell_at(c):
        return pl.ds(pl.multiple_of(c * CAP, CAP), CAP)

    def scaled(dom, c, extra):
        block = ext[dom, :, cell_at(c)]
        middle = jnp.where(comp == 0, centre[0] - (dom - 1.0), jnp.where(comp == 1, centre[1], centre[2]))
        u = (block - middle) * spread
        sq = u * u * -0.5
        n = sq[0:2] + sq[2:4] + sq[4:6] + extra
        return block, jnp.concatenate([u[0:6], n], axis=0)

    def prepare_far(dom):
        def body(c, carry):
            block, x = scaled(dom, c, 0.0)
            x1, x2, x3 = split3(x)
            z1 = jnp.where(rid < 6, x1, 1.0)
            z2 = jnp.where(rid < 6, x2, 1.0)
            cell = dom * cells + c
            kind = jnp.broadcast_to(block[6:7], (CAP, CAP))
            rows = jnp.concatenate([x1, x2, x3, z1, z2, z1, jnp.zeros((80, CAP), f32)], axis=0)
            far[cell, :, 0:CAP] = jnp.where(kind == subl, 1.0, 0.0).astype(bf16).T
            far[cell, :, CAP : 2 * CAP] = rows.astype(bf16).T
            q = jnp.concatenate([z1, jnp.where(rid < 6, x2, 0.0)], axis=0).astype(bf16)
            moment[cell, :, 0:CAP] = q
            moment[cell, :, CAP : 2 * CAP] = q
            return carry

        lax.fori_loop(0, cells, body, 0, unroll=prep_unroll)

    take[0].wait()
    prepare_far(1)

    def prepare_near(c, carry):
        block, x = scaled(1, c, log_scale)
        at = cell_at(c)
        for n in range(3):
            poso[n, :, at] = block[2 * n : 2 * n + 2]
        kindo[:, at] = block[6:7].astype(jnp.int32)
        x1, x2, x3 = split3(x)
        kind = jnp.broadcast_to(block[6:7], (CAP, CAP))
        onehot = jnp.where(kind == subl, 1.0, 0.0).astype(bf16)
        strength[c] = jnp.dot(table[...], onehot, preferred_element_type=f32).astype(bf16)
        for bead in range(2):
            mine = (rid < 6) & (parity == bead)
            norm = rid == 6 + bead
            y1 = jnp.where(mine, x1, jnp.where(norm, 1.0, 0.0))
            y12 = jnp.where(mine, x2, jnp.where(norm, x1, 0.0))
            y2 = jnp.where(mine | norm, x2, 0.0)
            y3 = jnp.where(mine | norm, x3, 0.0)
            near[c, :, bead * CAP : (bead + 1) * CAP] = jnp.concatenate([y1, y1, y1, y12, y2, y3], axis=0).astype(bf16)
        return carry

    lax.fori_loop(0, cells, prepare_near, 0, unroll=prep_unroll)
    give[0].start()
    give[1].start()
    for copy in take[1:]:
        copy.wait()
    prepare_far(0)
    prepare_far(2)
    near[cells] = jnp.zeros(near.shape[1:], bf16)
    strength[cells] = jnp.zeros(strength.shape[1:], bf16)
    total[...] = jnp.zeros(total.shape, f32)
    w1[...] = jnp.zeros(w1.shape, bf16)
    live_tiles = count[0]
    last = tiles.shape[1] - 1
    even = parity == 0

    def weigh(t, w, k):
        at = jnp.minimum(t, last)
        i = jnp.where(t < live_tiles, tiles[0, at], cells)
        j = tiles[1, at]
        s = jnp.dot(far[j, :, 0:CAP], strength[i], preferred_element_type=f32)
        e = jnp.dot(far[j, :, CAP : CAP + 48], near[i], preferred_element_type=f32)
        for bead in range(2):
            cut = slice(bead * CAP, (bead + 1) * CAP)
            weight = s * jnp.exp2(e[:, cut])
            high = weight.astype(bf16)
            w[k, 0:CAP, cut] = high
            w[k, CAP : 2 * CAP, cut] = (weight - high.astype(f32)).astype(bf16)

    def gather_force(t, w, k):
        at = jnp.clip(t, 0, last)
        i = jnp.where((t >= 0) & (t < live_tiles), tiles[0, at], cells)
        f = jnp.dot(moment[tiles[1, at]], w[k], preferred_element_type=f32)
        f = f[0:8] + f[8:16]
        total[i] += jnp.where(even, f[:, 0:CAP], f[:, CAP : 2 * CAP])

    def step(b, carry):
        base = b * 2 * batch
        for k in range(batch):
            weigh(base + k, w0, k)
            gather_force(base - batch + k, w1, k)
        for k in range(batch):
            weigh(base + batch + k, w1, k)
            gather_force(base + k, w0, k)
        return carry

    steps = (live_tiles + 2 * batch - 1) // (2 * batch)
    lax.fori_loop(0, steps, step, 0)
    for k in range(batch):
        gather_force(steps * 2 * batch - batch + k, w1, k)

    def finish(c, carry):
        block, x = scaled(1, c, 0.0)
        at = cell_at(c)
        r = total[c]
        got = (x * jnp.where(even, r[6:7], r[7:8]) - r) * (1.0 / spread)
        for n in range(3):
            pair = got[2 * n : 2 * n + 2]
            force[n, :, at] = pair
            momo[n, :, at] = mom[n, :, at] + inner_step * pair
        return carry

    lax.fori_loop(0, cells, finish, 0, unroll=prep_unroll)
    give[2].start()
    give[3].start()
    keep.wait()
    for copy in give:
        copy.wait()


def pair_forces(tiles, count, ext, mom, thermo, table):
    slots = ext.shape[2]
    cells = slots // CAP
    vm = pl.BlockSpec(memory_space=pltpu.VMEM)
    sm = pl.BlockSpec(memory_space=pltpu.SMEM)
    hbm = pl.BlockSpec(memory_space=pltpu.HBM)
    shape = jax.ShapeDtypeStruct
    beads = shape((3, 2, slots), f32)
    return pl.pallas_call(
        force_kernel,
        out_shape=(beads, beads, beads, shape((1, slots), jnp.int32), shape(thermo.shape, f32)),
        in_specs=[sm, sm, hbm, hbm, hbm, vm],
        out_specs=(hbm,) * 5,
        scratch_shapes=[
            pltpu.VMEM((3 * cells, CAP, 256), bf16),
            pltpu.VMEM((cells + 1, 48, 256), bf16),
            pltpu.VMEM((cells + 1, CAP, CAP), bf16),
            pltpu.VMEM((3 * cells, 16, 256), bf16),
            pltpu.VMEM((cells + 1, 8, CAP), f32),
            pltpu.VMEM((batch, 256, 256), bf16),
            pltpu.VMEM((batch, 256, 256), bf16),
            pltpu.VMEM((3, 8, slots), f32),
            *(pltpu.VMEM((3, 2, slots), f32) for _ in range(4)),
            pltpu.VMEM((1, slots), jnp.int32),
            pltpu.SemaphoreType.DMA((9,)),
        ],
        compiler_params=pltpu.CompilerParams(vmem_limit_bytes=56 * 2**20),
        name="pair_forces",
    )(tiles, count, ext, mom, thermo, table)


def per_device(peers, domains, positions, momenta, thermostat, atom_types, masses, pair_table,
               tile_pairs, tile_count, move_rows, move_count):
    slots = positions.shape[2]
    ext, moved, thermo = front(
        peers, domains, positions.transpose(1, 0, 2), momenta.transpose(1, 0, 2),
        thermostat.transpose(0, 2, 1, 3), atom_types.reshape(1, slots),
        masses.reshape(1, -1), move_rows[0], move_count)
    forces, momenta_out, positions_out, kinds, thermo_out = pair_forces(
        tile_pairs[0], tile_count, ext, moved, thermo, pair_table)
    return (
        positions_out.transpose(1, 0, 2), momenta_out.transpose(1, 0, 2),
        thermo_out.transpose(0, 2, 1, 3), forces.transpose(1, 0, 2), kinds.reshape(slots))


def solution(mesh):
    placed = (
        P("bead", None, "space"),
        P("bead", None, "space"),
        P("bead", None, None, "space"),
        P("space"),
        P(),
        P(),
        P("space", None, None),
        P("space"),
        P("space", None, None),
        P("space", None),
    )
    return jax.shard_map(
        functools.partial(per_device, mesh.shape["bead"], mesh.shape["space"]),
        mesh=mesh,
        in_specs=placed,
        out_specs=(
            P("bead", None, "space"),
            P("bead", None, "space"),
            P("bead", None, None, "space"),
            P("bead", None, "space"),
            P("space"),
        ),
        check_vma=False,
    )
```

```python
import functools
import math

import jax
import jax.numpy as jnp
import numpy as np
from jax import lax
from jax.experimental import pallas as pl
from jax.experimental.pallas import tpu as pltpu
from jax.sharding import PartitionSpec as P

NBEADS = 16
CAP = 128
CHAIN = 4
NTYPES = 128
outer_step = 0.2
inner_step = 0.05
thermal = 1.0
chain_mass = 2.0
cycle_freq = 2.0
pair_reach = 0.4
offsets = (1, -1, 2, -2)
opposite = (1, 0, 3, 2)
MESH = pl.DeviceIdType.MESH
f32 = jnp.float32
bf16 = jnp.bfloat16

reach2 = pair_reach * pair_reach
spread = math.sqrt(1.0 / (reach2 * math.log(2.0)))
log_scale = math.log2(1.0 / (reach2 * NBEADS))
centre = (0.5, 4.0, 3.0)
batch = 24
prep_unroll = 16


def split3(x):
    a = x.astype(bf16).astype(f32)
    b = (x - a).astype(bf16).astype(f32)
    return a, b, x - a - b


def cycle_map(peers):
    k = np.arange(NBEADS)
    w = 2.0 * cycle_freq * np.sin(math.pi * k / NBEADS)
    r = outer_step * w
    c = np.cos(r)
    s = np.where(k > 0, np.sin(r) / np.where(k > 0, w, 1.0), outer_step)
    b = -w * np.sin(r)
    lag = (k[:, None] - k[None, :]) % NBEADS
    phase = np.cos(2.0 * math.pi / NBEADS * (lag[:, :, None] * k % NBEADS))
    mc, ms, mb = ((phase * v).sum(2) / NBEADS for v in (c, s, b))
    maps = [[mc, ms], [mb, mc]]
    per = NBEADS // peers
    size = peers * 8
    big = np.zeros((3 * size, 3 * size))

    def place(p, kind, bead, comp, half):
        row = (kind * 3 + comp) * per + bead
        if row < 8:
            return half * size + p * 8 + row
        return 2 * size + p * 8 + half * 4 + row - 8

    for half in range(2):
        for comp in range(3):
            for kind in range(2):
                for kind2 in range(2):
                    for j in range(NBEADS):
                        for i in range(NBEADS):
                            to = place(j // per, kind, j % per, comp, half)
                            fro = place(i // per, kind2, i % per, comp, half)
                            big[to, fro] = maps[kind][kind2][j, i]
    small = np.zeros((3, size, size))
    for n, m in enumerate((mc, mb, ms)):
        for comp in range(3):
            for j in range(NBEADS):
                for i in range(NBEADS):
                    to = j // per * 8 + comp * per + j % per
                    small[n, to, i // per * 8 + comp * per + i % per] = m[j, i]
    return big.astype(np.float32), small.reshape(3 * size, size).astype(np.float32)


def front_kernel(
    peers, domains,
    pos_in, mom_in, thermo_in, types_in, masses_in, rows_in, count_in, big_in, small_in,
    ext_out, momo_out, tho_out,
    pos, mom, thermo, types, masses, rows, count, bigm, smallm,
    send1, recv1, send2, recv2, pth, mass, mask, into, picked, gat, sca,
    mig1, got1, mig2, got2, scale, e_out, e_in, ext, momo, tho,
    load, save, s1, r1, s2, r2, sm1, rm1, sm2, rm2, se, re, sh, rh,
):
    slots = pos.shape[2]
    chunk = slots // peers
    half = chunk // 2
    me_b = lax.axis_index("bead")
    me_s = lax.axis_index("space")

    def ring(off):
        return lax.rem(me_b + off + peers, peers)

    def domain(off):
        return lax.rem(me_s + off + domains, domains)

    def lanes(start, size):
        return pl.ds(pl.multiple_of(start, CAP), size)

    def class_offset(c):
        return (1 + c // 2) * (1 - 2 * (c % 2))

    pairs = [
        (types_in, types), (masses_in, masses), (pos_in, pos), (mom_in, mom), (thermo_in, thermo),
        (rows_in, rows), (count_in, count), (big_in, bigm), (small_in, smallm)]
    loads = [pltpu.make_async_copy(src, dst, load.at[n]) for n, (src, dst) in enumerate(pairs)]
    for copy in loads:
        copy.start()

    barrier = pltpu.get_barrier_semaphore()
    for off in range(1, peers):
        pl.semaphore_signal(barrier, inc=1, device_id=(ring(off), me_s), device_id_type=MESH)
    for off in offsets:
        pl.semaphore_signal(barrier, inc=1, device_id=(me_b, domain(off)), device_id_type=MESH)

    for q in range(peers):
        @pl.when(me_b != q)
        def _():
            pl.semaphore_signal(
                barrier, inc=1, device_id=(q, domain(-class_offset(q // 2))), device_id_type=MESH)

    for copy in loads[0:5]:
        copy.wait()
    m1, m2, m3 = split3(masses[...])
    mass_rows = jnp.concatenate([m1, m2, m3, jnp.zeros((5, NTYPES), f32)], axis=0).astype(bf16)
    kind_iota = lax.broadcasted_iota(jnp.int32, (NTYPES, chunk), 0)

    def chain(p):
        at = lanes(p * chunk, chunk)
        kind = types[:, at]
        onehot = jnp.where(jnp.broadcast_to(kind, (NTYPES, chunk)) == kind_iota, 1.0, 0.0).astype(bf16)
        found = jnp.dot(mass_rows, onehot, preferred_element_type=f32)
        found = found[0:1] + found[1:2] + found[2:3]
        mass[:, at] = found
        inv = 1.0 / found
        h = 0.5 * outer_step
        place = jnp.concatenate([pos[n, :, at] for n in range(3)], axis=0)
        q = jnp.concatenate([mom[n, :, at] for n in range(3)], axis=0)
        z = [
            jnp.concatenate([thermo[b, n, link : link + 1, at] for n in range(3) for b in range(2)], axis=0)
            for link in range(CHAIN)
        ]
        old = [q * q * inv * (1.0 / chain_mass)] + [v * v for v in z[:-1]]
        z[3] = z[3] + h * (old[3] - thermal / chain_mass)
        for link in (2, 1, 0):
            drive = old[link] - thermal / chain_mass
            z[link] = z[link] * jnp.exp(z[link + 1] * -h) + h * drive
        for link in range(CHAIN):
            pth[6 * link : 6 * link + 6, at] = z[link]
        vel = q * jnp.exp(z[0] * -h) * inv
        none = jnp.zeros((2, chunk), f32)
        pth[24:32, at] = jnp.concatenate([kind.astype(f32), found, none, none, none], axis=0)
        pth[32:40, at] = jnp.concatenate([place, none], axis=0)
        pth[40:48, at] = jnp.concatenate([vel, none], axis=0)
        send1[p, 0:6, 0:chunk] = place
        send1[p, 6:8, 0:chunk] = vel[0:2]
        for part in range(2):
            send1[p, 4 * part : 4 * part + 4, chunk : chunk + half] = vel[2:6, part * half : (part + 1) * half]

    def exchange(out, got, ssem, rsem, off):
        p = ring(off)
        return pltpu.make_async_remote_copy(
            src_ref=out.at[p], dst_ref=got.at[me_b], send_sem=ssem.at[off], recv_sem=rsem.at[off],
            device_id=(p, me_s), device_id_type=MESH)

    def arrival(out, got, ssem, rsem, off):
        p = ring(-off)
        return pltpu.make_async_remote_copy(
            src_ref=out.at[p], dst_ref=got.at[p], send_sem=ssem.at[off], recv_sem=rsem.at[off],
            device_id=(p, me_s), device_id_type=MESH)

    def far_first(step):
        k = (step + 1) // 2
        return peers // 2 + jnp.where(lax.rem(step, 2) == 1, -k, k)

    first = ring(far_first(0))
    chain(first)
    pl.semaphore_wait(barrier, 2 * (peers - 1) + len(offsets))
    exchange(send1, recv1, s1, r1, far_first(0)).start()

    def send_chunk(step, carry):
        off = far_first(step)
        chain(ring(off))
        exchange(send1, recv1, s1, r1, off).start()
        return carry

    lax.fori_loop(1, peers - 1, send_chunk, 0)
    chain(me_b)
    recv1[me_b] = send1[me_b]

    for copy in loads[5:]:
        copy.wait()
    into[...] = jnp.full(into.shape, -1.0, f32)
    into[0:4, 0 : rows.shape[1]] = rows[...].astype(f32)
    listed = into[0:4]
    spot = lax.broadcasted_iota(jnp.int32, (1, CAP), 1)
    for c in range(4):
        other = opposite[c]
        live = spot < jnp.broadcast_to(count[:, other : other + 1], (1, CAP))
        into[8 + c : 9 + c] = jnp.where(live, listed[other : other + 1], -1.0)
    landing = into[...].T
    picked[...] = jnp.zeros(picked.shape, f32)
    row_iota = lax.broadcasted_iota(jnp.int32, (CAP, CAP), 0).astype(f32).astype(bf16)
    one, zero = jnp.ones((CAP, CAP), bf16), jnp.zeros((CAP, CAP), bf16)

    def pick(n, carry):
        for k in range(chunk // CAP):
            local = (listed - (n * chunk + k * CAP).astype(f32)).astype(bf16)
            for c in range(4):
                gat[k * CAP : (k + 1) * CAP, c * CAP : (c + 1) * CAP] = jnp.where(
                    row_iota == jnp.broadcast_to(local[c : c + 1], (CAP, CAP)), one, zero)
        left = jnp.concatenate(split3(pth[:, lanes(n * chunk, chunk)]), axis=0).astype(bf16)
        picked[...] += jnp.dot(left, gat[...], preferred_element_type=f32)
        return carry

    lax.fori_loop(0, peers, pick, 0)
    leaving = picked[0:48] + picked[48:96] + picked[96:144]
    low = lax.broadcasted_iota(jnp.int32, (8, CAP), 1) < CAP // 2

    def swap(x):
        return pltpu.roll(x, CAP // 2, 1)

    for c in range(4):
        cut = slice(c * CAP, (c + 1) * CAP)
        place, vel = leaving[32:40, cut], leaving[40:48, cut]
        mig1[2 * c] = jnp.where(low, place, swap(vel))
        mig1[2 * c + 1] = jnp.where(low, swap(place), vel)
        m = jnp.broadcast_to(leaving[25:26, cut], (8, CAP))
        scale[2 * c] = jnp.where(low, 1.0, swap(m))
        scale[2 * c + 1] = jnp.where(low, 1.0, m)

    def send_leaving(step, carry):
        exchange(mig1, got1, sm1, rm1, far_first(step)).start()
        return carry

    lax.fori_loop(0, peers - 1, send_leaving, 0)
    got1[me_b] = mig1[me_b]

    def hop(out, got, ssem, rsem, c, to):
        return pltpu.make_async_remote_copy(
            src_ref=out.at[c], dst_ref=got.at[c], send_sem=ssem.at[c], recv_sem=rsem.at[c],
            device_id=(me_b, domain(to)), device_id_type=MESH)

    for c in range(4):
        e_out[c] = leaving[0:32, c * CAP : (c + 1) * CAP]
        hop(e_out, e_in, se, re, c, offsets[c]).start()

    def take1(off, carry):
        arrival(send1, recv1, s1, r1, off).wait_recv()
        return carry

    lax.fori_loop(1, peers, take1, 0)
    size = peers * 8
    right = jnp.concatenate(
        [recv1[:, :, n * half : (n + 1) * half].reshape(size, half) for n in range(3)], axis=0)
    mixed = jnp.dot(bigm[...], right, preferred_element_type=f32, precision=lax.Precision.HIGHEST)
    for n in range(3):
        send2[:, :, n * half : (n + 1) * half] = mixed[n * size : (n + 1) * size].reshape(peers, 8, half)

    def take_leaving(off, carry):
        arrival(mig1, got1, sm1, rm1, off).wait_recv()
        return carry

    lax.fori_loop(1, peers, take_leaving, 0)
    turned = jnp.dot(
        smallm[...], got1[...].reshape(size, CAP), preferred_element_type=f32,
        precision=lax.Precision.HIGHEST)
    low_all = lax.broadcasted_iota(jnp.int32, (size, CAP), 1) < CAP // 2
    cross = swap(jnp.where(low_all, turned[size : 2 * size], turned[2 * size : 3 * size]))
    mine = class_offset(me_b // 2)
    is_x = (lax.broadcasted_iota(jnp.int32, (8, CAP), 0) < 2) & low
    shift = jnp.where(is_x, mine.astype(f32), 0.0)
    mig2[...] = (turned[0:size] + cross).reshape(peers, 8, CAP) * scale[me_b][None] - shift[None]

    def deliver(p):
        return pltpu.make_async_remote_copy(
            src_ref=mig2.at[p], dst_ref=got2.at[me_b], send_sem=sm2.at[p], recv_sem=rm2.at[me_b],
            device_id=(p, domain(mine)), device_id_type=MESH)

    def delivered(q):
        return pltpu.make_async_remote_copy(
            src_ref=mig2.at[q], dst_ref=got2.at[q], send_sem=sm2.at[q], recv_sem=rm2.at[q],
            device_id=(q, domain(-mine)), device_id_type=MESH)

    def send_turned(p, carry):
        deliver(p).start()
        return carry

    def send_mixed(step, carry):
        exchange(send2, recv2, s2, r2, far_first(step)).start()
        return carry

    lax.fori_loop(0, peers, send_turned, 0)
    lax.fori_loop(0, peers - 1, send_mixed, 0)
    recv2[me_b] = send2[me_b]

    landed = [jnp.broadcast_to(landing[:, 8 + c : 9 + c], (CAP, CAP)) for c in range(4)]
    lane_iota = lax.broadcasted_iota(jnp.int32, (CAP, CAP), 1).astype(f32).astype(bf16)

    def land_map(n, carry):
        at = lanes(n * CAP, CAP)
        for c in range(4):
            local = (landed[c] - (n * CAP).astype(f32)).astype(bf16)
            sca[c * CAP : (c + 1) * CAP, at] = jnp.where(lane_iota == local, one, zero)
        return carry

    lax.fori_loop(0, slots // CAP, land_map, 0, unroll=2)


    for c in range(4):
        hop(e_out, e_in, se, re, c, -offsets[c]).wait_recv()
    x1, x2, x3 = split3(jnp.concatenate([e_in[c, 0:24] for c in range(4)], axis=1))
    kinds = jnp.concatenate([e_in[c, 24:32] for c in range(4)], axis=1)
    tag = lax.broadcasted_iota(jnp.int32, (8, 4 * CAP), 0)
    kinds = jnp.where(tag == 0, kinds, 1.0)
    early_left = jnp.concatenate([x1, x2, x3, kinds], axis=0).astype(bf16)

    def early_land(n, carry):
        at = lanes(n * 256, 256)
        new = jnp.dot(early_left, sca[:, at], preferred_element_type=f32)
        hit = new[73:74]
        mask[:, at] = hit
        merged = jnp.where(hit > 0.5, new[0:24] + new[24:48] + new[48:72], pth[0:24, at])
        for bead in range(2):
            for n in range(3):
                for link in range(CHAIN):
                    row = 6 * link + 2 * n + bead
                    tho[bead, n, link : link + 1, at] = merged[row : row + 1]
        ext[6:7, at] = jnp.where(hit > 0.5, new[72:73], pth[24:25, at])
        return carry

    ext[7:8] = jnp.zeros((1, slots), f32)
    lax.fori_loop(0, slots // 256, early_land, 0, unroll=2)
    chains = pltpu.make_async_copy(tho, tho_out, load.at[0])
    chains.start()

    def take_turned(q, carry):
        delivered(q).wait_recv()
        return carry

    lax.fori_loop(0, peers, take_turned, 0)
    came = [(got2[2 * c], got2[2 * c + 1]) for c in range(4)]
    place = jnp.concatenate([jnp.where(low, even, swap(odd)) for even, odd in came], axis=1)
    drift = jnp.concatenate([jnp.where(low, swap(even), odd) for even, odd in came], axis=1)
    late_left = jnp.concatenate(
        split3(jnp.concatenate([place, drift], axis=0)), axis=0).astype(bf16)

    def halo(side, p, to):
        cut = lanes(p * chunk, chunk)
        return pltpu.make_async_remote_copy(
            src_ref=ext.at[:, cut], dst_ref=ext_out.at[2 * side, :, cut],
            send_sem=sh.at[side, p], recv_sem=rh.at[side, p],
            device_id=(me_b, domain(to)), device_id_type=MESH)

    def keep(p):
        cut = lanes(p * chunk, chunk)
        return (
            pltpu.make_async_copy(ext.at[:, cut], ext_out.at[1, :, cut], save.at[0, p]),
            pltpu.make_async_copy(momo.at[:, :, cut], momo_out.at[:, :, cut], save.at[1, p]))

    def merge(p):
        at = lanes(p * chunk, chunk)
        new = jnp.dot(late_left, sca[:, at], preferred_element_type=f32)
        new = new[0:16] + new[16:32] + new[32:48]
        hit = mask[:, at] > 0.5
        m = mass[:, at]
        main = recv2[p, :, 0:chunk]
        rest = recv2[p, :, chunk : chunk + half]
        ext[0:6, at] = jnp.where(hit, new[0:6], main[0:6])
        halo(0, p, 1).start()
        halo(1, p, -1).start()
        drift = jnp.concatenate([main[6:8], jnp.concatenate([rest[0:4], rest[4:8]], axis=1)], axis=0)
        drift = jnp.where(hit, new[8:14], drift * m)
        for n in range(3):
            momo[n, :, at] = drift[2 * n : 2 * n + 2]
        for copy in keep(p):
            copy.start()

    merge(me_b)

    def take2(step, carry):
        off = far_first(peers - 2 - step)
        arrival(send2, recv2, s2, r2, off).wait_recv()
        merge(ring(-off))
        return carry

    lax.fori_loop(0, peers - 1, take2, 0)

    def drain(off, carry):
        exchange(send1, recv1, s1, r1, off).wait_send()
        exchange(send2, recv2, s2, r2, off).wait_send()
        exchange(mig1, got1, sm1, rm1, off).wait_send()
        return carry

    lax.fori_loop(1, peers, drain, 0)
    for c in range(4):
        hop(e_out, e_in, se, re, c, offsets[c]).wait_send()

    def take_halo(p, carry):
        deliver(p).wait_send()
        halo(0, p, 1).wait_send()
        halo(1, p, -1).wait_send()
        halo(0, p, -1).wait_recv()
        halo(1, p, 1).wait_recv()
        for copy in keep(p):
            copy.wait()
        return carry

    lax.fori_loop(0, peers, take_halo, 0)
    chains.wait()


def front(peers, domains, pos, mom, thermo, types, masses, rows, count):
    slots = pos.shape[2]
    chunk = slots // peers
    packed = chunk + chunk // 2
    bigm, smallm = (jnp.asarray(m) for m in cycle_map(peers))
    args = (pos, mom, thermo, types, masses, rows, count, bigm, smallm)
    hbm = pl.BlockSpec(memory_space=pltpu.HBM)
    dma = pltpu.SemaphoreType.DMA
    shape = jax.ShapeDtypeStruct
    block = pltpu.VMEM((peers, 8, packed), f32)
    small = pltpu.VMEM((peers, 8, CAP), f32)
    return pl.pallas_call(
        functools.partial(front_kernel, peers, domains),
        out_shape=(
            shape((3, 8, slots), f32),
            shape((3, 2, slots), f32),
            shape((2, 3, CHAIN, slots), f32),
        ),
        in_specs=[hbm] * len(args),
        out_specs=(hbm, hbm, hbm),
        scratch_shapes=[
            *(pltpu.VMEM(a.shape, a.dtype) for a in args),
            block, block, block, block,
            pltpu.VMEM((48, slots), f32),
            pltpu.VMEM((1, slots), f32),
            pltpu.VMEM((1, slots), f32),
            pltpu.VMEM((CAP, CAP), f32),
            pltpu.VMEM((144, 4 * CAP), f32),
            pltpu.VMEM((chunk, 4 * CAP), bf16),
            pltpu.VMEM((4 * CAP, slots), bf16),
            small, small, small, small, small,
            pltpu.VMEM((4, 32, CAP), f32),
            pltpu.VMEM((4, 32, CAP), f32),
            pltpu.VMEM((8, slots), f32),
            pltpu.VMEM((3, 2, slots), f32),
            pltpu.VMEM((2, 3, CHAIN, slots), f32),
            dma((len(args),)), dma((2, peers)),
            *(dma((peers,)) for _ in range(8)),
            dma((4,)), dma((4,)),
            dma((2, peers)), dma((2, peers)),
        ],
        compiler_params=pltpu.CompilerParams(
            collective_id=0, has_side_effects=True, vmem_limit_bytes=56 * 2**20),
        name="front",
    )(*args)


def force_kernel(
    tiles, count, ext_in, mom_in, thermo, table,
    force_out, momo_out, poso_out, kindo_out, tho,
    far, near, strength, moment, total, w0, w1, ext, mom, force, momo, poso, kindo, sem,
):
    slots = ext.shape[2]
    cells = slots // CAP
    take = [pltpu.make_async_copy(ext_in.at[d], ext.at[d], sem.at[d]) for d in (1, 0, 2)]
    take.append(pltpu.make_async_copy(mom_in, mom, sem.at[3]))
    keep = pltpu.make_async_copy(thermo, tho, sem.at[4])
    for copy in take:
        copy.start()
    keep.start()
    give = [
        pltpu.make_async_copy(src, dst, sem.at[5 + n])
        for n, (src, dst) in enumerate(
            [(poso, poso_out), (kindo, kindo_out), (force, force_out), (momo, momo_out)])]
    rid = lax.broadcasted_iota(jnp.int32, (8, CAP), 0)
    comp = rid // 2
    parity = lax.rem(rid, 2)
    subl = lax.broadcasted_iota(jnp.int32, (CAP, CAP), 0).astype(f32)

    def cell_at(c):
        return pl.ds(pl.multiple_of(c * CAP, CAP), CAP)

    def scaled(dom, c, extra):
        block = ext[dom, :, cell_at(c)]
        middle = jnp.where(comp == 0, centre[0] - (dom - 1.0), jnp.where(comp == 1, centre[1], centre[2]))
        u = (block - middle) * spread
        sq = u * u * -0.5
        n = sq[0:2] + sq[2:4] + sq[4:6] + extra
        return block, jnp.concatenate([u[0:6], n], axis=0)

    def prepare_far(dom):
        def body(c, carry):
            block, x = scaled(dom, c, 0.0)
            x1, x2, x3 = split3(x)
            z1 = jnp.where(rid < 6, x1, 1.0)
            z2 = jnp.where(rid < 6, x2, 1.0)
            cell = dom * cells + c
            kind = jnp.broadcast_to(block[6:7], (CAP, CAP))
            rows = jnp.concatenate([x1, x2, x3, z1, z2, z1, jnp.zeros((80, CAP), f32)], axis=0)
            far[cell, :, 0:CAP] = jnp.where(kind == subl, 1.0, 0.0).astype(bf16).T
            far[cell, :, CAP : 2 * CAP] = rows.astype(bf16).T
            q = jnp.concatenate([z1, jnp.where(rid < 6, x2, 0.0)], axis=0).astype(bf16)
            moment[cell, :, 0:CAP] = q
            moment[cell, :, CAP : 2 * CAP] = q
            return carry

        lax.fori_loop(0, cells, body, 0, unroll=prep_unroll)

    take[0].wait()
    prepare_far(1)

    def prepare_near(c, carry):
        block, x = scaled(1, c, log_scale)
        at = cell_at(c)
        for n in range(3):
            poso[n, :, at] = block[2 * n : 2 * n + 2]
        kindo[:, at] = block[6:7].astype(jnp.int32)
        x1, x2, x3 = split3(x)
        kind = jnp.broadcast_to(block[6:7], (CAP, CAP))
        onehot = jnp.where(kind == subl, 1.0, 0.0).astype(bf16)
        strength[c] = jnp.dot(table[...], onehot, preferred_element_type=f32).astype(bf16)
        for bead in range(2):
            mine = (rid < 6) & (parity == bead)
            norm = rid == 6 + bead
            y1 = jnp.where(mine, x1, jnp.where(norm, 1.0, 0.0))
            y12 = jnp.where(mine, x2, jnp.where(norm, x1, 0.0))
            y2 = jnp.where(mine | norm, x2, 0.0)
            y3 = jnp.where(mine | norm, x3, 0.0)
            near[c, :, bead * CAP : (bead + 1) * CAP] = jnp.concatenate([y1, y1, y1, y12, y2, y3], axis=0).astype(bf16)
        return carry

    lax.fori_loop(0, cells, prepare_near, 0, unroll=prep_unroll)
    give[0].start()
    give[1].start()
    for copy in take[1:]:
        copy.wait()
    prepare_far(0)
    prepare_far(2)
    near[cells] = jnp.zeros(near.shape[1:], bf16)
    strength[cells] = jnp.zeros(strength.shape[1:], bf16)
    total[...] = jnp.zeros(total.shape, f32)
    w1[...] = jnp.zeros(w1.shape, bf16)
    live_tiles = count[0]
    last = tiles.shape[1] - 1
    even = parity == 0

    def weigh(t, w, k):
        at = jnp.minimum(t, last)
        i = jnp.where(t < live_tiles, tiles[0, at], cells)
        j = tiles[1, at]
        s = jnp.dot(far[j, :, 0:CAP], strength[i], preferred_element_type=f32)
        e = jnp.dot(far[j, :, CAP : CAP + 48], near[i], preferred_element_type=f32)
        for bead in range(2):
            cut = slice(bead * CAP, (bead + 1) * CAP)
            weight = s * jnp.exp2(e[:, cut])
            high = weight.astype(bf16)
            w[k, 0:CAP, cut] = high
            w[k, CAP : 2 * CAP, cut] = (weight - high.astype(f32)).astype(bf16)

    def gather_force(t, w, k):
        at = jnp.clip(t, 0, last)
        i = jnp.where((t >= 0) & (t < live_tiles), tiles[0, at], cells)
        f = jnp.dot(moment[tiles[1, at]], w[k], preferred_element_type=f32)
        f = f[0:8] + f[8:16]
        total[i] += jnp.where(even, f[:, 0:CAP], f[:, CAP : 2 * CAP])

    def step(b, carry):
        base = b * 2 * batch
        for k in range(batch):
            weigh(base + k, w0, k)
            gather_force(base - batch + k, w1, k)
        for k in range(batch):
            weigh(base + batch + k, w1, k)
            gather_force(base + k, w0, k)
        return carry

    steps = (live_tiles + 2 * batch - 1) // (2 * batch)
    lax.fori_loop(0, steps, step, 0)
    for k in range(batch):
        gather_force(steps * 2 * batch - batch + k, w1, k)

    def finish(c, carry):
        block, x = scaled(1, c, 0.0)
        at = cell_at(c)
        r = total[c]
        got = (x * jnp.where(even, r[6:7], r[7:8]) - r) * (1.0 / spread)
        for n in range(3):
            pair = got[2 * n : 2 * n + 2]
            force[n, :, at] = pair
            momo[n, :, at] = mom[n, :, at] + inner_step * pair
        return carry

    lax.fori_loop(0, cells, finish, 0, unroll=prep_unroll)
    give[2].start()
    give[3].start()
    keep.wait()
    for copy in give:
        copy.wait()


def pair_forces(tiles, count, ext, mom, thermo, table):
    slots = ext.shape[2]
    cells = slots // CAP
    vm = pl.BlockSpec(memory_space=pltpu.VMEM)
    sm = pl.BlockSpec(memory_space=pltpu.SMEM)
    hbm = pl.BlockSpec(memory_space=pltpu.HBM)
    shape = jax.ShapeDtypeStruct
    beads = shape((3, 2, slots), f32)
    return pl.pallas_call(
        force_kernel,
        out_shape=(beads, beads, beads, shape((1, slots), jnp.int32), shape(thermo.shape, f32)),
        in_specs=[sm, sm, hbm, hbm, hbm, vm],
        out_specs=(hbm,) * 5,
        scratch_shapes=[
            pltpu.VMEM((3 * cells, CAP, 256), bf16),
            pltpu.VMEM((cells + 1, 48, 256), bf16),
            pltpu.VMEM((cells + 1, CAP, CAP), bf16),
            pltpu.VMEM((3 * cells, 16, 256), bf16),
            pltpu.VMEM((cells + 1, 8, CAP), f32),
            pltpu.VMEM((batch, 256, 256), bf16),
            pltpu.VMEM((batch, 256, 256), bf16),
            pltpu.VMEM((3, 8, slots), f32),
            *(pltpu.VMEM((3, 2, slots), f32) for _ in range(4)),
            pltpu.VMEM((1, slots), jnp.int32),
            pltpu.SemaphoreType.DMA((9,)),
        ],
        compiler_params=pltpu.CompilerParams(vmem_limit_bytes=56 * 2**20),
        name="pair_forces",
    )(tiles, count, ext, mom, thermo, table)


def per_device(peers, domains, positions, momenta, thermostat, atom_types, masses, pair_table,
               tile_pairs, tile_count, move_rows, move_count):
    slots = positions.shape[2]
    ext, moved, thermo = front(
        peers, domains, positions.transpose(1, 0, 2), momenta.transpose(1, 0, 2),
        thermostat.transpose(0, 2, 1, 3), atom_types.reshape(1, slots),
        masses.reshape(1, -1), move_rows[0], move_count)
    forces, momenta_out, positions_out, kinds, thermo_out = pair_forces(
        tile_pairs[0], tile_count, ext, moved, thermo, pair_table)
    return (
        positions_out.transpose(1, 0, 2), momenta_out.transpose(1, 0, 2),
        thermo_out.transpose(0, 2, 1, 3), forces.transpose(1, 0, 2), kinds.reshape(slots))


def solution(mesh):
    placed = (
        P("bead", None, "space"),
        P("bead", None, "space"),
        P("bead", None, None, "space"),
        P("space"),
        P(),
        P(),
        P("space", None, None),
        P("space"),
        P("space", None, None),
        P("space", None),
    )
    return jax.shard_map(
        functools.partial(per_device, mesh.shape["bead"], mesh.shape["space"]),
        mesh=mesh,
        in_specs=placed,
        out_specs=(
            P("bead", None, "space"),
            P("bead", None, "space"),
            P("bead", None, None, "space"),
            P("bead", None, "space"),
            P("space"),
        ),
        check_vma=False,
    )
```

```python
import functools
import math

import jax
import jax.numpy as jnp
import numpy as np
from jax import lax
from jax.experimental import pallas as pl
from jax.experimental.pallas import tpu as pltpu
from jax.sharding import PartitionSpec as P

NBEADS = 16
CAP = 128
CHAIN = 4
NTYPES = 128
outer_step = 0.2
inner_step = 0.05
thermal = 1.0
chain_mass = 2.0
cycle_freq = 2.0
pair_reach = 0.4
offsets = (1, -1, 2, -2)
opposite = (1, 0, 3, 2)
MESH = pl.DeviceIdType.MESH
f32 = jnp.float32
bf16 = jnp.bfloat16

reach2 = pair_reach * pair_reach
spread = math.sqrt(1.0 / (reach2 * math.log(2.0)))
log_scale = math.log2(1.0 / (reach2 * NBEADS))
centre = (0.5, 4.0, 3.0)
batch = 24
prep_unroll = 48


def split3(x):
    a = x.astype(bf16).astype(f32)
    b = (x - a).astype(bf16).astype(f32)
    return a, b, x - a - b


def cycle_map(peers):
    k = np.arange(NBEADS)
    w = 2.0 * cycle_freq * np.sin(math.pi * k / NBEADS)
    r = outer_step * w
    c = np.cos(r)
    s = np.where(k > 0, np.sin(r) / np.where(k > 0, w, 1.0), outer_step)
    b = -w * np.sin(r)
    lag = (k[:, None] - k[None, :]) % NBEADS
    phase = np.cos(2.0 * math.pi / NBEADS * (lag[:, :, None] * k % NBEADS))
    mc, ms, mb = ((phase * v).sum(2) / NBEADS for v in (c, s, b))
    maps = [[mc, ms], [mb, mc]]
    per = NBEADS // peers
    size = peers * 8
    big = np.zeros((3 * size, 3 * size))

    def place(p, kind, bead, comp, half):
        row = (kind * 3 + comp) * per + bead
        if row < 8:
            return half * size + p * 8 + row
        return 2 * size + p * 8 + half * 4 + row - 8

    for half in range(2):
        for comp in range(3):
            for kind in range(2):
                for kind2 in range(2):
                    for j in range(NBEADS):
                        for i in range(NBEADS):
                            to = place(j // per, kind, j % per, comp, half)
                            fro = place(i // per, kind2, i % per, comp, half)
                            big[to, fro] = maps[kind][kind2][j, i]
    small = np.zeros((3, size, size))
    for n, m in enumerate((mc, mb, ms)):
        for comp in range(3):
            for j in range(NBEADS):
                for i in range(NBEADS):
                    to = j // per * 8 + comp * per + j % per
                    small[n, to, i // per * 8 + comp * per + i % per] = m[j, i]
    return big.astype(np.float32), small.reshape(3 * size, size).astype(np.float32)


def front_kernel(
    peers, domains,
    pos_in, mom_in, thermo_in, types_in, masses_in, rows_in, count_in, big_in, small_in,
    ext_out, momo_out, tho_out,
    pos, mom, thermo, types, masses, rows, count, bigm, smallm,
    send1, recv1, send2, recv2, pth, mass, mask, into, picked, gat, sca,
    mig1, got1, mig2, got2, scale, e_out, e_in, ext, momo, tho,
    load, save, s1, r1, s2, r2, sm1, rm1, sm2, rm2, se, re, sh, rh,
):
    slots = pos.shape[2]
    chunk = slots // peers
    half = chunk // 2
    me_b = lax.axis_index("bead")
    me_s = lax.axis_index("space")

    def ring(off):
        return lax.rem(me_b + off + peers, peers)

    def domain(off):
        return lax.rem(me_s + off + domains, domains)

    def lanes(start, size):
        return pl.ds(pl.multiple_of(start, CAP), size)

    def class_offset(c):
        return (1 + c // 2) * (1 - 2 * (c % 2))

    pairs = [
        (types_in, types), (masses_in, masses), (pos_in, pos), (mom_in, mom), (thermo_in, thermo),
        (rows_in, rows), (count_in, count), (big_in, bigm), (small_in, smallm)]
    loads = [pltpu.make_async_copy(src, dst, load.at[n]) for n, (src, dst) in enumerate(pairs)]
    for copy in loads:
        copy.start()

    barrier = pltpu.get_barrier_semaphore()
    for off in range(1, peers):
        pl.semaphore_signal(barrier, inc=1, device_id=(ring(off), me_s), device_id_type=MESH)
    for off in offsets:
        pl.semaphore_signal(barrier, inc=1, device_id=(me_b, domain(off)), device_id_type=MESH)

    for q in range(peers):
        @pl.when(me_b != q)
        def _():
            pl.semaphore_signal(
                barrier, inc=1, device_id=(q, domain(-class_offset(q // 2))), device_id_type=MESH)

    for copy in loads[0:5]:
        copy.wait()
    m1, m2, m3 = split3(masses[...])
    mass_rows = jnp.concatenate([m1, m2, m3, jnp.zeros((5, NTYPES), f32)], axis=0).astype(bf16)
    kind_iota = lax.broadcasted_iota(jnp.int32, (NTYPES, chunk), 0)

    def chain(p):
        at = lanes(p * chunk, chunk)
        kind = types[:, at]
        onehot = jnp.where(jnp.broadcast_to(kind, (NTYPES, chunk)) == kind_iota, 1.0, 0.0).astype(bf16)
        found = jnp.dot(mass_rows, onehot, preferred_element_type=f32)
        found = found[0:1] + found[1:2] + found[2:3]
        mass[:, at] = found
        inv = 1.0 / found
        h = 0.5 * outer_step
        place = jnp.concatenate([pos[n, :, at] for n in range(3)], axis=0)
        q = jnp.concatenate([mom[n, :, at] for n in range(3)], axis=0)
        z = [
            jnp.concatenate([thermo[b, n, link : link + 1, at] for n in range(3) for b in range(2)], axis=0)
            for link in range(CHAIN)
        ]
        old = [q * q * inv * (1.0 / chain_mass)] + [v * v for v in z[:-1]]
        z[3] = z[3] + h * (old[3] - thermal / chain_mass)
        for link in (2, 1, 0):
            drive = old[link] - thermal / chain_mass
            z[link] = z[link] * jnp.exp(z[link + 1] * -h) + h * drive
        for link in range(CHAIN):
            pth[6 * link : 6 * link + 6, at] = z[link]
        vel = q * jnp.exp(z[0] * -h) * inv
        none = jnp.zeros((2, chunk), f32)
        pth[24:32, at] = jnp.concatenate([kind.astype(f32), found, none, none, none], axis=0)
        pth[32:40, at] = jnp.concatenate([place, none], axis=0)
        pth[40:48, at] = jnp.concatenate([vel, none], axis=0)
        send1[p, 0:6, 0:chunk] = place
        send1[p, 6:8, 0:chunk] = vel[0:2]
        for part in range(2):
            send1[p, 4 * part : 4 * part + 4, chunk : chunk + half] = vel[2:6, part * half : (part + 1) * half]

    def exchange(out, got, ssem, rsem, off):
        p = ring(off)
        return pltpu.make_async_remote_copy(
            src_ref=out.at[p], dst_ref=got.at[me_b], send_sem=ssem.at[off], recv_sem=rsem.at[off],
            device_id=(p, me_s), device_id_type=MESH)

    def arrival(out, got, ssem, rsem, off):
        p = ring(-off)
        return pltpu.make_async_remote_copy(
            src_ref=out.at[p], dst_ref=got.at[p], send_sem=ssem.at[off], recv_sem=rsem.at[off],
            device_id=(p, me_s), device_id_type=MESH)

    def far_first(step):
        k = (step + 1) // 2
        return peers // 2 + jnp.where(lax.rem(step, 2) == 1, -k, k)

    first = ring(far_first(0))
    chain(first)
    pl.semaphore_wait(barrier, 2 * (peers - 1) + len(offsets))
    exchange(send1, recv1, s1, r1, far_first(0)).start()

    def send_chunk(step, carry):
        off = far_first(step)
        chain(ring(off))
        exchange(send1, recv1, s1, r1, off).start()
        return carry

    lax.fori_loop(1, peers - 1, send_chunk, 0)
    chain(me_b)
    recv1[me_b] = send1[me_b]

    for copy in loads[5:]:
        copy.wait()
    into[...] = jnp.full(into.shape, -1.0, f32)
    into[0:4, 0 : rows.shape[1]] = rows[...].astype(f32)
    listed = into[0:4]
    spot = lax.broadcasted_iota(jnp.int32, (1, CAP), 1)
    for c in range(4):
        other = opposite[c]
        live = spot < jnp.broadcast_to(count[:, other : other + 1], (1, CAP))
        into[8 + c : 9 + c] = jnp.where(live, listed[other : other + 1], -1.0)
    landing = into[...].T
    picked[...] = jnp.zeros(picked.shape, f32)
    row_iota = lax.broadcasted_iota(jnp.int32, (CAP, CAP), 0).astype(f32).astype(bf16)
    one, zero = jnp.ones((CAP, CAP), bf16), jnp.zeros((CAP, CAP), bf16)

    def pick(n, carry):
        for k in range(chunk // CAP):
            local = (listed - (n * chunk + k * CAP).astype(f32)).astype(bf16)
            for c in range(4):
                gat[k * CAP : (k + 1) * CAP, c * CAP : (c + 1) * CAP] = jnp.where(
                    row_iota == jnp.broadcast_to(local[c : c + 1], (CAP, CAP)), one, zero)
        left = jnp.concatenate(split3(pth[:, lanes(n * chunk, chunk)]), axis=0).astype(bf16)
        picked[...] += jnp.dot(left, gat[...], preferred_element_type=f32)
        return carry

    lax.fori_loop(0, peers, pick, 0)
    leaving = picked[0:48] + picked[48:96] + picked[96:144]
    low = lax.broadcasted_iota(jnp.int32, (8, CAP), 1) < CAP // 2

    def swap(x):
        return pltpu.roll(x, CAP // 2, 1)

    for c in range(4):
        cut = slice(c * CAP, (c + 1) * CAP)
        place, vel = leaving[32:40, cut], leaving[40:48, cut]
        mig1[2 * c] = jnp.where(low, place, swap(vel))
        mig1[2 * c + 1] = jnp.where(low, swap(place), vel)
        m = jnp.broadcast_to(leaving[25:26, cut], (8, CAP))
        scale[2 * c] = jnp.where(low, 1.0, swap(m))
        scale[2 * c + 1] = jnp.where(low, 1.0, m)

    def send_leaving(step, carry):
        exchange(mig1, got1, sm1, rm1, far_first(step)).start()
        return carry

    lax.fori_loop(0, peers - 1, send_leaving, 0)
    got1[me_b] = mig1[me_b]

    def hop(out, got, ssem, rsem, c, to):
        return pltpu.make_async_remote_copy(
            src_ref=out.at[c], dst_ref=got.at[c], send_sem=ssem.at[c], recv_sem=rsem.at[c],
            device_id=(me_b, domain(to)), device_id_type=MESH)

    for c in range(4):
        e_out[c] = leaving[0:32, c * CAP : (c + 1) * CAP]
        hop(e_out, e_in, se, re, c, offsets[c]).start()

    def take1(off, carry):
        arrival(send1, recv1, s1, r1, off).wait_recv()
        return carry

    lax.fori_loop(1, peers, take1, 0)
    size = peers * 8
    right = jnp.concatenate(
        [recv1[:, :, n * half : (n + 1) * half].reshape(size, half) for n in range(3)], axis=0)
    mixed = jnp.dot(bigm[...], right, preferred_element_type=f32, precision=lax.Precision.HIGHEST)
    for n in range(3):
        send2[:, :, n * half : (n + 1) * half] = mixed[n * size : (n + 1) * size].reshape(peers, 8, half)

    def take_leaving(off, carry):
        arrival(mig1, got1, sm1, rm1, off).wait_recv()
        return carry

    lax.fori_loop(1, peers, take_leaving, 0)
    turned = jnp.dot(
        smallm[...], got1[...].reshape(size, CAP), preferred_element_type=f32,
        precision=lax.Precision.HIGHEST)
    low_all = lax.broadcasted_iota(jnp.int32, (size, CAP), 1) < CAP // 2
    cross = swap(jnp.where(low_all, turned[size : 2 * size], turned[2 * size : 3 * size]))
    mine = class_offset(me_b // 2)
    is_x = (lax.broadcasted_iota(jnp.int32, (8, CAP), 0) < 2) & low
    shift = jnp.where(is_x, mine.astype(f32), 0.0)
    mig2[...] = (turned[0:size] + cross).reshape(peers, 8, CAP) * scale[me_b][None] - shift[None]

    def deliver(p):
        return pltpu.make_async_remote_copy(
            src_ref=mig2.at[p], dst_ref=got2.at[me_b], send_sem=sm2.at[p], recv_sem=rm2.at[me_b],
            device_id=(p, domain(mine)), device_id_type=MESH)

    def delivered(q):
        return pltpu.make_async_remote_copy(
            src_ref=mig2.at[q], dst_ref=got2.at[q], send_sem=sm2.at[q], recv_sem=rm2.at[q],
            device_id=(q, domain(-mine)), device_id_type=MESH)

    def send_turned(p, carry):
        deliver(p).start()
        return carry

    def send_mixed(step, carry):
        exchange(send2, recv2, s2, r2, far_first(step)).start()
        return carry

    lax.fori_loop(0, peers, send_turned, 0)
    lax.fori_loop(0, peers - 1, send_mixed, 0)
    recv2[me_b] = send2[me_b]

    landed = [jnp.broadcast_to(landing[:, 8 + c : 9 + c], (CAP, CAP)) for c in range(4)]
    lane_iota = lax.broadcasted_iota(jnp.int32, (CAP, CAP), 1).astype(f32).astype(bf16)

    def land_map(n, carry):
        at = lanes(n * CAP, CAP)
        for c in range(4):
            local = (landed[c] - (n * CAP).astype(f32)).astype(bf16)
            sca[c * CAP : (c + 1) * CAP, at] = jnp.where(lane_iota == local, one, zero)
        return carry

    lax.fori_loop(0, slots // CAP, land_map, 0, unroll=2)


    for c in range(4):
        hop(e_out, e_in, se, re, c, -offsets[c]).wait_recv()
    x1, x2, x3 = split3(jnp.concatenate([e_in[c, 0:24] for c in range(4)], axis=1))
    kinds = jnp.concatenate([e_in[c, 24:32] for c in range(4)], axis=1)
    tag = lax.broadcasted_iota(jnp.int32, (8, 4 * CAP), 0)
    kinds = jnp.where(tag == 0, kinds, 1.0)
    early_left = jnp.concatenate([x1, x2, x3, kinds], axis=0).astype(bf16)

    def early_land(n, carry):
        at = lanes(n * 256, 256)
        new = jnp.dot(early_left, sca[:, at], preferred_element_type=f32)
        hit = new[73:74]
        mask[:, at] = hit
        merged = jnp.where(hit > 0.5, new[0:24] + new[24:48] + new[48:72], pth[0:24, at])
        for bead in range(2):
            for n in range(3):
                for link in range(CHAIN):
                    row = 6 * link + 2 * n + bead
                    tho[bead, n, link : link + 1, at] = merged[row : row + 1]
        ext[6:7, at] = jnp.where(hit > 0.5, new[72:73], pth[24:25, at])
        return carry

    ext[7:8] = jnp.zeros((1, slots), f32)
    lax.fori_loop(0, slots // 256, early_land, 0, unroll=2)
    chains = pltpu.make_async_copy(tho, tho_out, load.at[0])
    chains.start()

    def take_turned(q, carry):
        delivered(q).wait_recv()
        return carry

    lax.fori_loop(0, peers, take_turned, 0)
    came = [(got2[2 * c], got2[2 * c + 1]) for c in range(4)]
    place = jnp.concatenate([jnp.where(low, even, swap(odd)) for even, odd in came], axis=1)
    drift = jnp.concatenate([jnp.where(low, swap(even), odd) for even, odd in came], axis=1)
    late_left = jnp.concatenate(
        split3(jnp.concatenate([place, drift], axis=0)), axis=0).astype(bf16)

    def halo(side, p, to):
        cut = lanes(p * chunk, chunk)
        return pltpu.make_async_remote_copy(
            src_ref=ext.at[:, cut], dst_ref=ext_out.at[2 * side, :, cut],
            send_sem=sh.at[side, p], recv_sem=rh.at[side, p],
            device_id=(me_b, domain(to)), device_id_type=MESH)

    def keep(p):
        cut = lanes(p * chunk, chunk)
        return (
            pltpu.make_async_copy(ext.at[:, cut], ext_out.at[1, :, cut], save.at[0, p]),
            pltpu.make_async_copy(momo.at[:, :, cut], momo_out.at[:, :, cut], save.at[1, p]))

    def merge(p):
        at = lanes(p * chunk, chunk)
        new = jnp.dot(late_left, sca[:, at], preferred_element_type=f32)
        new = new[0:16] + new[16:32] + new[32:48]
        hit = mask[:, at] > 0.5
        m = mass[:, at]
        main = recv2[p, :, 0:chunk]
        rest = recv2[p, :, chunk : chunk + half]
        ext[0:6, at] = jnp.where(hit, new[0:6], main[0:6])
        halo(0, p, 1).start()
        halo(1, p, -1).start()
        drift = jnp.concatenate([main[6:8], jnp.concatenate([rest[0:4], rest[4:8]], axis=1)], axis=0)
        drift = jnp.where(hit, new[8:14], drift * m)
        for n in range(3):
            momo[n, :, at] = drift[2 * n : 2 * n + 2]
        for copy in keep(p):
            copy.start()

    merge(me_b)

    def take2(step, carry):
        off = far_first(peers - 2 - step)
        arrival(send2, recv2, s2, r2, off).wait_recv()
        merge(ring(-off))
        return carry

    lax.fori_loop(0, peers - 1, take2, 0)

    def drain(off, carry):
        exchange(send1, recv1, s1, r1, off).wait_send()
        exchange(send2, recv2, s2, r2, off).wait_send()
        exchange(mig1, got1, sm1, rm1, off).wait_send()
        return carry

    lax.fori_loop(1, peers, drain, 0)
    for c in range(4):
        hop(e_out, e_in, se, re, c, offsets[c]).wait_send()

    def take_halo(p, carry):
        deliver(p).wait_send()
        halo(0, p, 1).wait_send()
        halo(1, p, -1).wait_send()
        halo(0, p, -1).wait_recv()
        halo(1, p, 1).wait_recv()
        for copy in keep(p):
            copy.wait()
        return carry

    lax.fori_loop(0, peers, take_halo, 0)
    chains.wait()


def front(peers, domains, pos, mom, thermo, types, masses, rows, count):
    slots = pos.shape[2]
    chunk = slots // peers
    packed = chunk + chunk // 2
    bigm, smallm = (jnp.asarray(m) for m in cycle_map(peers))
    args = (pos, mom, thermo, types, masses, rows, count, bigm, smallm)
    hbm = pl.BlockSpec(memory_space=pltpu.HBM)
    dma = pltpu.SemaphoreType.DMA
    shape = jax.ShapeDtypeStruct
    block = pltpu.VMEM((peers, 8, packed), f32)
    small = pltpu.VMEM((peers, 8, CAP), f32)
    return pl.pallas_call(
        functools.partial(front_kernel, peers, domains),
        out_shape=(
            shape((3, 8, slots), f32),
            shape((3, 2, slots), f32),
            shape((2, 3, CHAIN, slots), f32),
        ),
        in_specs=[hbm] * len(args),
        out_specs=(hbm, hbm, hbm),
        scratch_shapes=[
            *(pltpu.VMEM(a.shape, a.dtype) for a in args),
            block, block, block, block,
            pltpu.VMEM((48, slots), f32),
            pltpu.VMEM((1, slots), f32),
            pltpu.VMEM((1, slots), f32),
            pltpu.VMEM((CAP, CAP), f32),
            pltpu.VMEM((144, 4 * CAP), f32),
            pltpu.VMEM((chunk, 4 * CAP), bf16),
            pltpu.VMEM((4 * CAP, slots), bf16),
            small, small, small, small, small,
            pltpu.VMEM((4, 32, CAP), f32),
            pltpu.VMEM((4, 32, CAP), f32),
            pltpu.VMEM((8, slots), f32),
            pltpu.VMEM((3, 2, slots), f32),
            pltpu.VMEM((2, 3, CHAIN, slots), f32),
            dma((len(args),)), dma((2, peers)),
            *(dma((peers,)) for _ in range(8)),
            dma((4,)), dma((4,)),
            dma((2, peers)), dma((2, peers)),
        ],
        compiler_params=pltpu.CompilerParams(
            collective_id=0, has_side_effects=True, vmem_limit_bytes=56 * 2**20),
        name="front",
    )(*args)


def force_kernel(
    tiles, count, ext_in, mom_in, thermo, table,
    force_out, momo_out, poso_out, kindo_out, tho,
    far, near, strength, moment, total, w0, w1, ext, mom, force, momo, poso, kindo, sem,
):
    slots = ext.shape[2]
    cells = slots // CAP
    take = [pltpu.make_async_copy(ext_in.at[d], ext.at[d], sem.at[d]) for d in (1, 0, 2)]
    take.append(pltpu.make_async_copy(mom_in, mom, sem.at[3]))
    keep = pltpu.make_async_copy(thermo, tho, sem.at[4])
    for copy in take:
        copy.start()
    keep.start()
    give = [
        pltpu.make_async_copy(src, dst, sem.at[5 + n])
        for n, (src, dst) in enumerate(
            [(poso, poso_out), (kindo, kindo_out), (force, force_out), (momo, momo_out)])]
    rid = lax.broadcasted_iota(jnp.int32, (8, CAP), 0)
    comp = rid // 2
    parity = lax.rem(rid, 2)
    subl = lax.broadcasted_iota(jnp.int32, (CAP, CAP), 0).astype(f32)

    def cell_at(c):
        return pl.ds(pl.multiple_of(c * CAP, CAP), CAP)

    def scaled(dom, c, extra):
        block = ext[dom, :, cell_at(c)]
        middle = jnp.where(comp == 0, centre[0] - (dom - 1.0), jnp.where(comp == 1, centre[1], centre[2]))
        u = (block - middle) * spread
        sq = u * u * -0.5
        n = sq[0:2] + sq[2:4] + sq[4:6] + extra
        return block, jnp.concatenate([u[0:6], n], axis=0)

    def prepare_far(dom):
        def body(c, carry):
            block, x = scaled(dom, c, 0.0)
            x1, x2, x3 = split3(x)
            z1 = jnp.where(rid < 6, x1, 1.0)
            z2 = jnp.where(rid < 6, x2, 1.0)
            cell = dom * cells + c
            kind = jnp.broadcast_to(block[6:7], (CAP, CAP))
            rows = jnp.concatenate([x1, x2, x3, z1, z2, z1, jnp.zeros((80, CAP), f32)], axis=0)
            far[cell, :, 0:CAP] = jnp.where(kind == subl, 1.0, 0.0).astype(bf16).T
            far[cell, :, CAP : 2 * CAP] = rows.astype(bf16).T
            q = jnp.concatenate([z1, jnp.where(rid < 6, x2, 0.0)], axis=0).astype(bf16)
            moment[cell, :, 0:CAP] = q
            moment[cell, :, CAP : 2 * CAP] = q
            return carry

        lax.fori_loop(0, cells, body, 0, unroll=prep_unroll)

    take[0].wait()
    prepare_far(1)

    def prepare_near(c, carry):
        block, x = scaled(1, c, log_scale)
        at = cell_at(c)
        for n in range(3):
            poso[n, :, at] = block[2 * n : 2 * n + 2]
        kindo[:, at] = block[6:7].astype(jnp.int32)
        x1, x2, x3 = split3(x)
        kind = jnp.broadcast_to(block[6:7], (CAP, CAP))
        onehot = jnp.where(kind == subl, 1.0, 0.0).astype(bf16)
        strength[c] = jnp.dot(table[...], onehot, preferred_element_type=f32).astype(bf16)
        for bead in range(2):
            mine = (rid < 6) & (parity == bead)
            norm = rid == 6 + bead
            y1 = jnp.where(mine, x1, jnp.where(norm, 1.0, 0.0))
            y12 = jnp.where(mine, x2, jnp.where(norm, x1, 0.0))
            y2 = jnp.where(mine | norm, x2, 0.0)
            y3 = jnp.where(mine | norm, x3, 0.0)
            near[c, :, bead * CAP : (bead + 1) * CAP] = jnp.concatenate([y1, y1, y1, y12, y2, y3], axis=0).astype(bf16)
        return carry

    lax.fori_loop(0, cells, prepare_near, 0, unroll=prep_unroll)
    give[0].start()
    give[1].start()
    for copy in take[1:]:
        copy.wait()
    prepare_far(0)
    prepare_far(2)
    near[cells] = jnp.zeros(near.shape[1:], bf16)
    strength[cells] = jnp.zeros(strength.shape[1:], bf16)
    total[...] = jnp.zeros(total.shape, f32)
    w1[...] = jnp.zeros(w1.shape, bf16)
    live_tiles = count[0]
    last = tiles.shape[1] - 1
    even = parity == 0

    def weigh(t, w, k):
        at = jnp.minimum(t, last)
        i = jnp.where(t < live_tiles, tiles[0, at], cells)
        j = tiles[1, at]
        s = jnp.dot(far[j, :, 0:CAP], strength[i], preferred_element_type=f32)
        e = jnp.dot(far[j, :, CAP : CAP + 48], near[i], preferred_element_type=f32)
        for bead in range(2):
            cut = slice(bead * CAP, (bead + 1) * CAP)
            weight = s * jnp.exp2(e[:, cut])
            high = weight.astype(bf16)
            w[k, 0:CAP, cut] = high
            w[k, CAP : 2 * CAP, cut] = (weight - high.astype(f32)).astype(bf16)

    def gather_force(t, w, k):
        at = jnp.clip(t, 0, last)
        i = jnp.where((t >= 0) & (t < live_tiles), tiles[0, at], cells)
        f = jnp.dot(moment[tiles[1, at]], w[k], preferred_element_type=f32)
        f = f[0:8] + f[8:16]
        total[i] += jnp.where(even, f[:, 0:CAP], f[:, CAP : 2 * CAP])

    def step(b, carry):
        base = b * 2 * batch
        for k in range(batch):
            weigh(base + k, w0, k)
            gather_force(base - batch + k, w1, k)
        for k in range(batch):
            weigh(base + batch + k, w1, k)
            gather_force(base + k, w0, k)
        return carry

    steps = (live_tiles + 2 * batch - 1) // (2 * batch)
    lax.fori_loop(0, steps, step, 0)
    for k in range(batch):
        gather_force(steps * 2 * batch - batch + k, w1, k)

    def finish(c, carry):
        block, x = scaled(1, c, 0.0)
        at = cell_at(c)
        r = total[c]
        got = (x * jnp.where(even, r[6:7], r[7:8]) - r) * (1.0 / spread)
        for n in range(3):
            pair = got[2 * n : 2 * n + 2]
            force[n, :, at] = pair
            momo[n, :, at] = mom[n, :, at] + inner_step * pair
        return carry

    lax.fori_loop(0, cells, finish, 0, unroll=prep_unroll)
    give[2].start()
    give[3].start()
    keep.wait()
    for copy in give:
        copy.wait()


def pair_forces(tiles, count, ext, mom, thermo, table):
    slots = ext.shape[2]
    cells = slots // CAP
    vm = pl.BlockSpec(memory_space=pltpu.VMEM)
    sm = pl.BlockSpec(memory_space=pltpu.SMEM)
    hbm = pl.BlockSpec(memory_space=pltpu.HBM)
    shape = jax.ShapeDtypeStruct
    beads = shape((3, 2, slots), f32)
    return pl.pallas_call(
        force_kernel,
        out_shape=(beads, beads, beads, shape((1, slots), jnp.int32), shape(thermo.shape, f32)),
        in_specs=[sm, sm, hbm, hbm, hbm, vm],
        out_specs=(hbm,) * 5,
        scratch_shapes=[
            pltpu.VMEM((3 * cells, CAP, 256), bf16),
            pltpu.VMEM((cells + 1, 48, 256), bf16),
            pltpu.VMEM((cells + 1, CAP, CAP), bf16),
            pltpu.VMEM((3 * cells, 16, 256), bf16),
            pltpu.VMEM((cells + 1, 8, CAP), f32),
            pltpu.VMEM((batch, 256, 256), bf16),
            pltpu.VMEM((batch, 256, 256), bf16),
            pltpu.VMEM((3, 8, slots), f32),
            *(pltpu.VMEM((3, 2, slots), f32) for _ in range(4)),
            pltpu.VMEM((1, slots), jnp.int32),
            pltpu.SemaphoreType.DMA((9,)),
        ],
        compiler_params=pltpu.CompilerParams(vmem_limit_bytes=56 * 2**20),
        name="pair_forces",
    )(tiles, count, ext, mom, thermo, table)


def per_device(peers, domains, positions, momenta, thermostat, atom_types, masses, pair_table,
               tile_pairs, tile_count, move_rows, move_count):
    slots = positions.shape[2]
    ext, moved, thermo = front(
        peers, domains, positions.transpose(1, 0, 2), momenta.transpose(1, 0, 2),
        thermostat.transpose(0, 2, 1, 3), atom_types.reshape(1, slots),
        masses.reshape(1, -1), move_rows[0], move_count)
    forces, momenta_out, positions_out, kinds, thermo_out = pair_forces(
        tile_pairs[0], tile_count, ext, moved, thermo, pair_table)
    return (
        positions_out.transpose(1, 0, 2), momenta_out.transpose(1, 0, 2),
        thermo_out.transpose(0, 2, 1, 3), forces.transpose(1, 0, 2), kinds.reshape(slots))


def solution(mesh):
    placed = (
        P("bead", None, "space"),
        P("bead", None, "space"),
        P("bead", None, None, "space"),
        P("space"),
        P(),
        P(),
        P("space", None, None),
        P("space"),
        P("space", None, None),
        P("space", None),
    )
    return jax.shard_map(
        functools.partial(per_device, mesh.shape["bead"], mesh.shape["space"]),
        mesh=mesh,
        in_specs=placed,
        out_specs=(
            P("bead", None, "space"),
            P("bead", None, "space"),
            P("bead", None, None, "space"),
            P("bead", None, "space"),
            P("space"),
        ),
        check_vma=False,
    )
```
